512 devices in a mesh: seq: 64 (over z, y_lo, core), mp: 8 (over y_hi, x).
Axes of the slice: x: 4, y: 4 (y_hi: 2, y_lo: 2; y = y_hi * 2 + y_lo), z: 16, core: 2. Of those that a mesh axis runs over, the one named last changes fastest.
Arguments:
- layer_input: bfloat16 [16384, 8192], P('seq', 'mp'), may hold values from -8 to 8
- query_heads: bfloat16 [16384, 1024], P('seq', 'mp'), may hold values from -100 to 100
- key_head: bfloat16 [16384, 128], P('seq'), may hold values from -5 to 5
- value_head: bfloat16 [16384, 128], P('seq'), may hold values from -6 to 6
- attn_grad: bfloat16 [16384, 1024], P('seq', 'mp'), may hold values from -6 to 6
- block_order: int32 [128], replicated, may hold values from 0 to 127, as said below
- owners: int32 [8, 64], P('mp'), may hold values from 0 to 63, each once within a row
Outputs:
- query_grad: bfloat16 [16384, 1024], P('seq', 'mp')
- grad_blocks: float32 [8, 64, 64, 64], P('mp', 'seq')
- left_stats: float32 [8, 64, 64, 64], P('mp', 'seq')
- right_stats: float32 [8, 64, 64, 64], P('mp', 'seq')
The draws below stay inside these ranges and needn't reach their ends.
Inputs may be any that keep to these rules, and one draw needn't show every extreme that they name: `block_order`: storage block 2 s + 1 holds position block 127 minus the position block of storage block 2 s; the position blocks of storage blocks 0, 2, 4, ... run cyclically through 0 to 63, upward or downward, from a drawn start. `owners`: each row is a permutation.
All inputs are finite; a program needn't handle non-finite values.
Results may differ from the reference program's by a relative error of at most 0.009.
Values may be sent and summed in bfloat16 or wider, within the bound.
A program may use at most 64 MiB of HBM per device.

```python
import math
import jax
import jax.numpy as jnp
from jax import lax

D = 8192
HEADS = 8
HD = 128
HALF = 128
W = 2
BLK = 64
GROUPS = 8
NBLOCKS = 128
TOKENS = 16384
SPAN = 256
NBLK_MP = 64
N_MP = 8


def shared_keys(key):
    base = jnp.clip(jax.random.normal(jax.random.fold_in(key, 8), (TOKENS, HD), jnp.float32), -4.5, 4.5)
    return base


def draw_key_head(key, part):
    base = shared_keys(key)
    return base.astype(jnp.bfloat16)


def draw_query_heads(key, part):
    key = jax.random.fold_in(key, 1)
    queries = jnp.clip(jax.random.normal(key, (TOKENS, HEADS * HD), jnp.float32), -4.5, 4.5)
    return queries.astype(jnp.bfloat16)


def draw_block_order(key, part):
    key = jax.random.fold_in(key, 3)
    pairs = NBLOCKS // 2
    start = jax.random.randint(jax.random.fold_in(key, 1), (), 0, pairs)
    flipped = jax.random.randint(jax.random.fold_in(key, 2), (), 0, 2)
    places = jnp.arange(pairs, dtype=jnp.int32)
    steps = jnp.where(flipped == 1, -places, places)
    first = (steps + start) % pairs
    return jnp.stack([first, NBLOCKS - 1 - first], 1).reshape(NBLOCKS).astype(jnp.int32)


def raised(result, own_key, source, target, parts, factor):
    def block_of(dim):
        return (jnp.arange(result.shape[dim]) // (result.shape[dim] // parts)).reshape((-1,) + (1,) * (result.ndim - 1 - dim))

    near = jax.random.permutation(own_key, parts)[block_of(target)]
    second = (block_of(target) + parts // 2) % parts
    return jnp.where((block_of(source) == near) | (block_of(source) == second), factor * result, result)


def steps_of(own_key, shape, cuts, low, high):
    gain, own = 1.0, jax.random.fold_in(own_key, 6)
    for position, shards_of in cuts:
        draws = jnp.exp(jax.random.uniform(jax.random.fold_in(own, position), (shards_of,), jnp.float32, low / len(cuts), high / len(cuts)))
        gain = gain * jnp.repeat(draws, shape[position] // shards_of).reshape([-1 if axis == position else 1 for axis in range(len(shape))])
    return gain


def gaussian(own_key, extent, width, bound, cuts=(), kind=jnp.bfloat16):
    result = jax.random.normal(own_key, extent, jnp.float32) * width
    if len(cuts) > 0:
        result = steps_of(own_key, extent, cuts, -0.22, 0.18) * result
    return jnp.clip(result, min=-bound, max=bound).astype(kind)


def bell_draw_with(rng, dims, deviation, bound, cuts, heavy, kind=jnp.bfloat16):
    drawn = deviation * jax.random.normal(rng, dims, jnp.float32)
    if cuts:
        drawn = drawn * steps_of(rng, dims, cuts, -0.22, 0.18)
    return jnp.clip(raised(drawn, jax.random.fold_in(rng, 3), *heavy), -bound, bound).astype(kind)


def setup_inputs(seed: int = 0) -> dict:
    seeds = jax.random.split(jax.random.key(seed), 8)
    layer_input = bell_draw_with(seeds[0], (TOKENS, D), 1.0, 8.0, ((0, 64), (1, 8)), (0, 1, 64, 4.0))
    query_heads = draw_query_heads(jax.random.fold_in(seeds[7], 71), 0)
    key_head = draw_key_head(jax.random.fold_in(seeds[7], 71), 0)
    value_head = gaussian(seeds[3], (TOKENS, HD), 1.0, 6.0, ((0, 64),))
    attn_grad = gaussian(seeds[4], (TOKENS, HEADS * HD), 1.0, 6.0, ((0, 64), (1, 8)))
    block_order = draw_block_order(jax.random.fold_in(seeds[7], 71), 0)
    owners = jax.vmap(lambda own: jax.random.permutation(own, NBLK_MP))(jax.random.split(seeds[6], GROUPS)).reshape((GROUPS, NBLK_MP)).astype(jnp.int32)
    return {"layer_input": layer_input, "query_heads": query_heads, "key_head": key_head, "value_head": value_head, "attn_grad": attn_grad, "block_order": block_order, "owners": owners}


MASKED = -1e+30

def reference(layer_input, query_heads, key_head, value_head, attn_grad, block_order, owners):
    block_count = TOKENS // HALF
    score_scale = 1.0 / math.sqrt(HD)

    def to_position(array):
        pieces = array.reshape(block_count, HALF, array.shape[-1])
        return jnp.zeros_like(pieces).at[block_order].set(pieces)
    query_pos = to_position(query_heads).reshape(block_count, HALF, HEADS, HD)
    grad_pos = to_position(attn_grad).reshape(block_count, HALF, HEADS, HD)
    key_pos = to_position(key_head)
    value_pos = to_position(value_head)
    padding = jnp.zeros((W, HALF, HD), key_head.dtype)
    key_padded = jnp.concatenate([padding, key_pos], 0)
    value_padded = jnp.concatenate([padding, value_pos], 0)
    key_window = jnp.stack([key_padded[slot:slot + block_count] for slot in range(W + 1)], 1).reshape(block_count, (W + 1) * HALF, HD)
    value_window = jnp.stack([value_padded[slot:slot + block_count] for slot in range(W + 1)], 1).reshape(block_count, (W + 1) * HALF, HD)
    relative = jnp.arange((W + 1) * HALF, dtype=jnp.int32) - W * HALF
    in_block = jnp.arange(HALF, dtype=jnp.int32)

    def one_block(inputs):
        block, queries, grads, keys, values = inputs
        apart = in_block[:, None] - relative[None, :]
        visible = (apart >= 0) & (apart < SPAN) & (block * HALF + relative[None, :] >= 0)
        q_full = queries.astype(jnp.float32)
        g_full = grads.astype(jnp.float32)
        k_full = keys.astype(jnp.float32)
        v_full = values.astype(jnp.float32)
        scores = jnp.einsum('qhd,kd->hqk', q_full, k_full) * score_scale
        scores = jnp.where(visible[None], scores, MASKED)
        row_top = lax.optimization_barrier(jnp.max(scores, -1, keepdims=True))
        log_total = row_top + jnp.log(lax.optimization_barrier(jnp.sum(jnp.exp(scores - row_top), -1, keepdims=True)))
        prob = jnp.exp(scores - log_total)
        prob_b = lax.optimization_barrier(prob.astype(jnp.bfloat16)).astype(jnp.float32)
        attended = jnp.einsum('hqk,kd->qhd', prob_b, v_full)
        delta = lax.optimization_barrier(jnp.sum(g_full * attended, -1))
        dprob = jnp.einsum('qhd,kd->hqk', g_full, v_full)
        dscore = prob * (dprob - delta.T[:, :, None])
        dscore_b = lax.optimization_barrier(dscore.astype(jnp.bfloat16)).astype(jnp.float32)
        query_grad = jnp.einsum('hqk,kd->qhd', dscore_b, k_full) * score_scale
        key_grad = jnp.einsum('hqk,qhd->kd', dscore_b, q_full) * score_scale
        value_grad = jnp.einsum('hqk,qhd->kd', prob_b, g_full)
        return (query_grad, key_grad, value_grad)
    blocks = jnp.arange(block_count, dtype=jnp.int32)
    query_grad, key_window_grad, value_window_grad = lax.map(one_block, (blocks, query_pos, grad_pos, key_window, value_window))
    key_window_grad = key_window_grad.reshape(block_count, W + 1, HALF, HD)
    value_window_grad = value_window_grad.reshape(block_count, W + 1, HALF, HD)
    key_total = jnp.zeros((block_count + W, HALF, HD), jnp.float32)
    value_total = jnp.zeros((block_count + W, HALF, HD), jnp.float32)
    for slot in range(W + 1):
        key_total = key_total.at[slot:slot + block_count].add(key_window_grad[:, slot])
        value_total = value_total.at[slot:slot + block_count].add(value_window_grad[:, slot])
    kv_grad = jnp.concatenate([key_total[W:].reshape(TOKENS, HD), value_total[W:].reshape(TOKENS, HD)], 1).astype(jnp.bfloat16)
    input_pos = to_position(layer_input).reshape(TOKENS, D)
    weight_grad = jnp.dot(input_pos.T, kv_grad, preferred_element_type=jnp.float32) * (1.0 / math.sqrt(TOKENS))
    query_out = query_grad[block_order].reshape(TOKENS, HEADS * HD).astype(jnp.bfloat16)
    pieces = weight_grad.reshape(N_MP, D // N_MP // BLK, BLK, 2 * HD // BLK, BLK)
    pieces = pieces.transpose(0, 1, 3, 2, 4).reshape(N_MP, NBLK_MP, BLK, BLK)
    arranged = jax.vmap(lambda group, order: jnp.zeros_like(group).at[order].set(group))(pieces, owners)
    left_stats = jnp.einsum('mbij,mbkj->mbik', arranged, arranged, precision=lax.Precision.HIGHEST) / BLK
    right_stats = jnp.einsum('mbji,mbjk->mbik', arranged, arranged, precision=lax.Precision.HIGHEST) / BLK
    return (query_out, arranged, left_stats, right_stats)
```

```python
import functools
import math

import jax
import jax.numpy as jnp
from jax import lax
from jax.experimental import pallas as pl
from jax.experimental.pallas import tpu as pltpu
from jax.sharding import PartitionSpec as P

BLK = 64
MASKED = -1e30
MESH = pl.DeviceIdType.MESH
F32 = jnp.float32
BF16 = jnp.bfloat16


def contract(a, b, dims):
    return lax.dot_general(a, b, (dims, ((), ())), preferred_element_type=F32)


def kernel(
    n_seq,
    n_mp,
    order_ref,
    owners_ref,
    x_hbm,
    q_ref,
    k_ref,
    v_ref,
    g_ref,
    qg_ref,
    gb_ref,
    left_ref,
    right_ref,
    x_v,
    xt_v,
    inv_v,
    inv_s,
    kv_own,
    kv_in,
    kv_far,
    terms,
    terms_own,
    terms_in,
    pass_near,
    pass_far,
    pass_near_in,
    pass_far_in,
    fin,
    kvg,
    pieces,
    keep,
    core_out,
    core_in,
    y_out,
    y_in,
    z_sum,
    z_out,
    z_in,
    local_sem,
    kv_send,
    kv_recv,
    rs_send,
    rs_recv,
    pass_send,
    pass_recv,
    ag_send,
    ag_recv,
    pair_send,
    pair_recv,
    z_send,
    z_recv,
):
    n_z = n_seq // 4
    rows = q_ref.shape[0]
    half = rows // 2
    hd = q_ref.shape[1]
    cut = half // n_mp
    n_blocks = pieces.shape[0]
    score_scale = 1.0 / math.sqrt(hd)

    s = lax.axis_index("seq")
    m = lax.axis_index("mp")
    core = lax.rem(s, 2)
    y = lax.rem(s // 2, 2)
    z = s // 4

    def place(distance):
        return lax.rem(s + distance + n_seq, n_seq)

    def mate(t):
        return lax.rem(m + t, n_mp)

    x_copy = pltpu.make_async_copy(x_hbm, x_v, local_sem.at[0])
    x_copy.start()

    barrier = pltpu.get_barrier_semaphore()
    partners = [(place(d), m) for d in (1, -1, 2, -2)]
    partners += [(s, mate(t)) for t in range(1, n_mp)]
    partners += [(place(4 * t), m) for t in range(1, n_z)]
    for partner in partners:
        pl.semaphore_signal(barrier, inc=1, device_id=partner, device_id_type=MESH)

    first = order_ref[2 * s]
    following = order_ref[2 * place(1)]
    up = ((following - first + n_seq) & (n_seq - 1)) == 1
    last = first == n_seq - 1
    second_last = first == n_seq - 2

    for slot in range(2):
        kv_own[slot, :, :hd] = k_ref[slot * half : (slot + 1) * half, :]
        kv_own[slot, :, hd:] = v_ref[slot * half : (slot + 1) * half, :]
    kv_far[0] = kv_own[jnp.where(up, 0, 1)]
    kv_far[1] = kv_own[jnp.where(up, 1, 0)]

    pl.semaphore_wait(barrier, len(partners))

    def remote(src, dst, send_sem, recv_sem, to):
        copy = pltpu.make_async_remote_copy(
            src_ref=src,
            dst_ref=dst,
            send_sem=send_sem,
            recv_sem=recv_sem,
            device_id=to,
            device_id_type=MESH,
        )
        copy.start()
        return copy

    started = []
    kv_copies = [
        remote(kv_own, kv_in.at[0:2], kv_send.at[0], kv_recv.at[0], (place(1), m)),
        remote(kv_own, kv_in.at[2:4], kv_send.at[1], kv_recv.at[1], (place(-1), m)),
        remote(kv_far.at[0], kv_in.at[4], kv_send.at[2], kv_recv.at[2], (place(2), m)),
        remote(kv_far.at[1], kv_in.at[5], kv_send.at[3], kv_recv.at[3], (place(-2), m)),
    ]
    started += kv_copies

    spread = jnp.broadcast_to(owners_ref[...], (n_blocks, n_blocks)).T
    slot_of = lax.broadcasted_iota(jnp.int32, (n_blocks, n_blocks), 1)
    block_of = lax.broadcasted_iota(jnp.int32, (n_blocks, n_blocks), 0)
    inv_v[...] = jnp.max(jnp.where(spread == slot_of, block_of, 0), 0, keepdims=True)
    inv_copy = pltpu.make_async_copy(inv_v, inv_s, local_sem.at[1])
    inv_copy.start()

    x_copy.wait()
    xt_v[...] = x_v[...].T
    inv_copy.wait()

    for copy in kv_copies:
        copy.wait_recv()

    row = lax.broadcasted_iota(jnp.int32, (half, half), 0)
    col = lax.broadcasted_iota(jnp.int32, (half, half), 1)
    near_down = jnp.where(up, 0, 2)
    near_up = jnp.where(up, 2, 0)
    before = [
        (kv_in[near_down], kv_in[jnp.where(up, 4, 5)]),
        (
            jnp.where(last, kv_own[0], kv_in[near_up + 1]),
            kv_in[jnp.where(last, near_down, jnp.where(second_last, near_up, jnp.where(up, 5, 4)))],
        ),
    ]
    for slot in range(2):
        window = jnp.concatenate([kv_own[slot], *before[slot]], 0)
        keys, values = window[:, :hd], window[:, hd:]
        queries = q_ref[slot * half : (slot + 1) * half, :]
        grads = g_ref[slot * half : (slot + 1) * half, :]
        position = first if slot == 0 else 2 * n_seq - 1 - first
        visible = jnp.concatenate(
            [
                row - col >= 0,
                jnp.broadcast_to(position >= 1, (half, half)),
                (row - col < 0) & (position >= 2),
            ],
            1,
        )
        scores = jnp.where(visible, contract(queries, keys, ((1,), (1,))) * score_scale, MASKED)
        dprob = contract(grads, values, ((1,), (1,)))
        top = jnp.max(scores, -1, keepdims=True)
        raw = jnp.exp(scores - top)
        prob = raw * (1.0 / jnp.sum(raw, -1, keepdims=True))
        prob_b = prob.astype(BF16)
        delta = jnp.sum(prob_b.astype(F32) * dprob, -1, keepdims=True)
        dscore = (prob * (dprob - delta)).astype(BF16)
        value_grad = contract(prob_b, grads, ((0,), (0,)))
        key_grad = contract(dscore, queries, ((0,), (0,))) * score_scale
        qg_ref[slot * half : (slot + 1) * half, :] = (
            contract(dscore, keys, ((1,), (0,))) * score_scale
        ).astype(BF16)
        for part, index in enumerate((slot, 2 + 2 * slot, 3 + 2 * slot)):
            here = slice(part * half, (part + 1) * half)
            terms_own[index, :, :hd] = key_grad[here]
            terms_own[index, :, hd:] = value_grad[here]
            terms[index, :, :hd] = key_grad[here].astype(BF16)
            terms[index, :, hd:] = value_grad[here].astype(BF16)

    rs_copies = [
        remote(
            terms.at[:, pl.ds(pl.multiple_of(mate(t) * cut, cut), cut), :],
            terms_in.at[t - 1],
            rs_send.at[t - 1],
            rs_recv.at[t - 1],
            (s, mate(t)),
        )
        for t in range(1, n_mp)
    ]
    started += rs_copies
    my_rows = pl.ds(pl.multiple_of(m * cut, cut), cut)
    total = terms_own[:, my_rows, :]
    for t in range(1, n_mp):
        rs_copies[t - 1].wait_recv()
        total = total + terms_in[t - 1].astype(F32)

    own0, own1, down1, down2, up1, up2 = [total[i] for i in range(6)]
    own0 = own0 + jnp.where(last, up1, 0.0)
    down1 = down1 + jnp.where(last, up2, 0.0)
    up1 = jnp.where(last, 0.0, up1)
    crossing = jnp.where(second_last, up2, 0.0)
    up2 = jnp.where(last | second_last, 0.0, up2)
    nothing = jnp.zeros_like(own0)
    pass_near[0, 0] = jnp.where(up, crossing, down1).astype(BF16)
    pass_near[0, 1] = jnp.where(up, up1, nothing).astype(BF16)
    pass_near[1, 0] = jnp.where(up, down1, crossing).astype(BF16)
    pass_near[1, 1] = jnp.where(up, nothing, up1).astype(BF16)
    pass_far[0] = jnp.where(up, up2, down2).astype(BF16)
    pass_far[1] = jnp.where(up, down2, up2).astype(BF16)
    pass_copies = [
        remote(pass_near.at[0], pass_near_in.at[0], pass_send.at[0], pass_recv.at[0], (place(1), m)),
        remote(pass_near.at[1], pass_near_in.at[1], pass_send.at[1], pass_recv.at[1], (place(-1), m)),
        remote(pass_far.at[0], pass_far_in.at[0], pass_send.at[2], pass_recv.at[2], (place(2), m)),
        remote(pass_far.at[1], pass_far_in.at[1], pass_send.at[3], pass_recv.at[3], (place(-2), m)),
    ]
    started += pass_copies
    for copy in pass_copies:
        copy.wait_recv()
    from_before = pass_far_in[0].astype(F32)
    from_after = pass_far_in[1].astype(F32)
    near = pass_near_in[0].astype(F32) + pass_near_in[1].astype(F32)
    own0 = own0 + near[0] + jnp.where(up, from_after, from_before)
    own1 = own1 + near[1] + jnp.where(up, from_before, from_after)
    fin[0] = own0.astype(BF16)
    fin[1] = own1.astype(BF16)
    kvg[:, my_rows, :] = fin[...]
    ag_copies = [
        remote(fin, kvg.at[:, my_rows, :], ag_send.at[t - 1], ag_recv.at[t - 1], (s, mate(t)))
        for t in range(1, n_mp)
    ]
    started += ag_copies
    for copy in ag_copies:
        copy.wait_recv()

    kv_grad = kvg[...].reshape(rows, 2 * hd)
    lane = lax.broadcasted_iota(jnp.int32, (BLK // 2, 2 * BLK), 1)
    weight_scale = 1.0 / math.sqrt(rows * n_seq)
    step = min(4, n_blocks // 4)

    @pl.loop(0, n_blocks // (4 * step))
    def _(i):
        here = pl.ds(pl.multiple_of(i * step * BLK, step * BLK), step * BLK)
        part = contract(xt_v[here, :], kv_grad, ((1,), (0,))) * weight_scale
        for r in range(step):
            for j in range(2):
                tile = part[r * BLK : (r + 1) * BLK, j * 2 * BLK : (j + 1) * 2 * BLK]
                upper, lower = tile[: BLK // 2], tile[BLK // 2 :]
                pieces[(i * step + r) * 4 + 2 * j] = jnp.where(
                    lane < BLK, upper, pltpu.roll(lower, BLK, 1)
                )
                pieces[(i * step + r) * 4 + 2 * j + 1] = jnp.where(
                    lane < BLK, pltpu.roll(upper, BLK, 1), lower
                )

    @pl.loop(0, 2 * n_z)
    def _(j):
        slot = 2 * (2 * lax.rem(j, n_z) + j // n_z)
        core_out[j] = pieces[inv_s[0, slot + 1 - core] & (n_blocks - 1)].astype(BF16)

    core_copy = remote(core_out, core_in, pair_send.at[0], pair_recv.at[0], (s + 1 - 2 * core, m))
    started.append(core_copy)

    @pl.loop(0, 2 * n_z)
    def _(j):
        slot = 2 * (2 * lax.rem(j, n_z) + j // n_z)
        keep[j] = pieces[inv_s[0, slot + core] & (n_blocks - 1)]

    core_copy.wait_recv()
    theirs = pl.ds((1 - y) * n_z, n_z)
    y_out[...] = (keep[theirs] + core_in[theirs].astype(F32)).astype(BF16)
    y_copy = remote(y_out, y_in, pair_send.at[1], pair_recv.at[1], (s + 2 - 4 * y, m))
    started.append(y_copy)
    ours = pl.ds(y * n_z, n_z)
    z_sum[...] = keep[ours] + core_in[ours].astype(F32)
    y_copy.wait_recv()
    z_sum[...] += y_in[...].astype(F32)
    z_out[...] = z_sum[...].astype(BF16)
    z_copies = [
        remote(
            z_out.at[lax.rem(z + t, n_z)],
            z_in.at[t - 1],
            z_send.at[t - 1],
            z_recv.at[t - 1],
            (place(4 * t), m),
        )
        for t in range(1, n_z)
    ]
    started += z_copies
    owned = z_sum[z]
    for t in range(1, n_z):
        z_copies[t - 1].wait_recv()
        owned = owned + z_in[t - 1].astype(F32)

    block = jnp.concatenate([owned[:, :BLK], owned[:, BLK:]], 0)
    gb_ref[0, 0] = block

    def exact(dims):
        return (
            lax.dot_general(
                block,
                block,
                (dims, ((), ())),
                precision=lax.Precision.HIGHEST,
                preferred_element_type=F32,
            )
            / BLK
        )

    left_ref[0, 0] = exact(((1,), (1,)))
    right_ref[0, 0] = exact(((0,), (0,)))
    for copy in started:
        copy.wait_send()


def shards(n_seq, n_mp, layer_input, query_heads, key_head, value_head, attn_grad, block_order, owners):
    rows, columns = layer_input.shape
    half = rows // 2
    hd = key_head.shape[1]
    cut = half // n_mp
    n_z = n_seq // 4
    n_blocks = owners.shape[1]
    shape = (BLK // 2, 2 * BLK)
    vmem = pl.BlockSpec(memory_space=pltpu.VMEM)
    stat = jax.ShapeDtypeStruct((1, 1, BLK, BLK), F32)
    dma = pltpu.SemaphoreType.DMA
    return pl.pallas_call(
        functools.partial(kernel, n_seq, n_mp),
        out_shape=(jax.ShapeDtypeStruct((rows, hd), BF16), stat, stat, stat),
        in_specs=[
            pl.BlockSpec(memory_space=pltpu.SMEM),
            vmem,
            pl.BlockSpec(memory_space=pl.ANY),
            vmem,
            vmem,
            vmem,
            vmem,
        ],
        out_specs=(vmem, vmem, vmem, vmem),
        scratch_shapes=[
            pltpu.VMEM((rows, columns), BF16),
            pltpu.VMEM((columns, rows), BF16),
            pltpu.VMEM((1, n_blocks), jnp.int32),
            pltpu.SMEM((1, n_blocks), jnp.int32),
            pltpu.VMEM((2, half, 2 * hd), BF16),
            pltpu.VMEM((6, half, 2 * hd), BF16),
            pltpu.VMEM((2, half, 2 * hd), BF16),
            pltpu.VMEM((6, half, 2 * hd), BF16),
            pltpu.VMEM((6, half, 2 * hd), F32),
            pltpu.VMEM((n_mp - 1, 6, cut, 2 * hd), BF16),
            pltpu.VMEM((2, 2, cut, 2 * hd), BF16),
            pltpu.VMEM((2, cut, 2 * hd), BF16),
            pltpu.VMEM((2, 2, cut, 2 * hd), BF16),
            pltpu.VMEM((2, cut, 2 * hd), BF16),
            pltpu.VMEM((2, cut, 2 * hd), BF16),
            pltpu.VMEM((2, half, 2 * hd), BF16),
            pltpu.VMEM((n_blocks, *shape), F32),
            pltpu.VMEM((2 * n_z, *shape), F32),
            pltpu.VMEM((2 * n_z, *shape), BF16),
            pltpu.VMEM((2 * n_z, *shape), BF16),
            pltpu.VMEM((n_z, *shape), BF16),
            pltpu.VMEM((n_z, *shape), BF16),
            pltpu.VMEM((n_z, *shape), F32),
            pltpu.VMEM((n_z, *shape), BF16),
            pltpu.VMEM((n_z - 1, *shape), BF16),
            dma((2,)),
            dma((4,)),
            dma((4,)),
            dma((n_mp - 1,)),
            dma((n_mp - 1,)),
            dma((4,)),
            dma((4,)),
            dma((n_mp - 1,)),
            dma((n_mp - 1,)),
            dma((2,)),
            dma((2,)),
            dma((n_z - 1,)),
            dma((n_z - 1,)),
        ],
        compiler_params=pltpu.CompilerParams(
            collective_id=0, has_side_effects=True, vmem_limit_bytes=32 * 1024 * 1024
        ),
    )(block_order, owners, layer_input, query_heads, key_head, value_head, attn_grad)


def solution(mesh):
    return jax.shard_map(
        functools.partial(shards, mesh.shape["seq"], mesh.shape["mp"]),
        mesh=mesh,
        in_specs=(
            P("seq", "mp"),
            P("seq", "mp"),
            P("seq", None),
            P("seq", None),
            P("seq", "mp"),
            P(),
            P("mp", None),
        ),
        out_specs=(
            P("seq", "mp"),
            P("mp", "seq", None, None),
            P("mp", "seq", None, None),
            P("mp", "seq", None, None),
        ),
        check_vma=False,
    )
```

```python
import functools
import math

import jax
import jax.numpy as jnp
from jax import lax
from jax.experimental import pallas as pl
from jax.experimental.pallas import tpu as pltpu
from jax.sharding import PartitionSpec as P

BLK = 64
STEP = 4
PARTS = 4
MASKED = -1e30
MESH = pl.DeviceIdType.MESH
F32 = jnp.float32
BF16 = jnp.bfloat16


def contract(a, b, dims):
    return lax.dot_general(a, b, (dims, ((), ())), preferred_element_type=F32)


def kernel(
    n_seq,
    n_mp,
    order_hbm,
    owners_hbm,
    x_hbm,
    q_hbm,
    k_hbm,
    v_hbm,
    g_hbm,
    qg_ref,
    sum_ref,
    order_ref,
    owners_ref,
    q_ref,
    g_ref,
    x_v,
    xt_v,
    inv_v,
    inv_s,
    kv_own,
    kv_sel,
    kv_in,
    kv_other,
    terms,
    terms_own,
    terms_in,
    pass_near,
    pass_far,
    pass_near_in,
    pass_far_in,
    fin,
    kvg,
    pieces,
    keep,
    core_out,
    core_in,
    y_out,
    y_in,
    z_out,
    z_in,
    load_sem,
    word_sem,
    kv_send,
    kv_recv,
    rs_send,
    rs_recv,
    pass_send,
    pass_recv,
    ag_send,
    ag_recv,
    core_send,
    core_recv,
    y_send,
    y_recv,
    z_send,
    z_recv,
):
    n_z = n_seq // 4
    rows = q_ref.shape[0]
    half = rows // 2
    hd = q_ref.shape[1]
    cut = half // n_mp
    n_blocks = pieces.shape[0]
    score_scale = 1.0 / math.sqrt(hd)

    s = lax.axis_index("seq")
    m = lax.axis_index("mp")
    core = lax.rem(s, 2)
    y = lax.rem(s // 2, 2)
    z = s // 4

    def place(distance):
        return lax.rem(s + distance + n_seq, n_seq)

    n_x = min(4, n_mp)
    offsets = sorted(
        [(a, b) for a in range(n_mp // n_x) for b in range(n_x) if a + b > 0],
        key=lambda o: -(2 * o[0] + min(o[1], n_x - o[1])),
    )

    def mate(offset):
        a, b = offset
        return lax.rem(m // n_x + a, n_mp // n_x) * n_x + lax.rem(lax.rem(m, n_x) + b, n_x)

    loads = [
        pltpu.make_async_copy(src, dst, load_sem.at[i])
        for i, (src, dst) in enumerate(
            [
                (order_hbm, order_ref),
                (k_hbm.at[0:half], kv_own.at[0, 0]),
                (v_hbm.at[0:half], kv_own.at[0, 1]),
                (k_hbm.at[half:rows], kv_own.at[1, 0]),
                (v_hbm.at[half:rows], kv_own.at[1, 1]),
                (owners_hbm, owners_ref),
                (q_hbm, q_ref),
                (g_hbm, g_ref),
                (x_hbm, x_v),
            ]
        )
    ]
    for load in loads:
        load.start()

    barrier = pltpu.get_barrier_semaphore()
    next_x = sorted({(0, 1), (0, n_x - 1)} - {(0, 0)})
    all_x = [(0, b) for b in range(1, n_x)]
    other_y = [(a, 0) for a in range(1, n_mp // n_x)]
    next_z = [(place(4 * t), m) for t in sorted({1, n_z - 1})]
    partners = [(place(d), m) for d in (1, -1, 2, -2)] + next_z
    partners += [(s, mate(o)) for o in next_x + other_y]
    reaches = [1 << i for i in range((n_z // 2).bit_length() - 1)]
    along_z = [[(place(4 * t), m) for t in (r, n_z - r)] for r in reaches[1:]]
    rounds = [partners, [(s, mate(o)) for o in all_x] + sum(along_z[:1], []), *along_z[1:]]

    def tell(i):
        for partner in rounds[i]:
            pl.semaphore_signal(
                word_sem.at[i], inc=1, device_id=partner, device_id_type=MESH
            )

    def heard(i):
        pl.semaphore_wait(word_sem.at[i], len(rounds[i]))

    for partner in partners:
        pl.semaphore_signal(barrier, inc=1, device_id=partner, device_id_type=MESH)

    for load in loads[:5]:
        load.wait()

    first = order_ref[2 * s]
    following = order_ref[2 * place(1)]
    up = ((following - first + n_seq) & (n_seq - 1)) == 1
    last = first == n_seq - 1
    second_last = first == n_seq - 2

    kv_sel[0] = kv_own[jnp.where(up, 0, 1)]
    kv_sel[1] = kv_own[jnp.where(up, 1, 0)]

    pl.semaphore_wait(barrier, len(partners))

    def remote(src, dst, send_sem, recv_sem, to):
        copy = pltpu.make_async_remote_copy(
            src_ref=src,
            dst_ref=dst,
            send_sem=send_sem,
            recv_sem=recv_sem,
            device_id=to,
            device_id_type=MESH,
        )
        copy.start()
        return copy

    started = []
    kv_copies = [
        remote(kv_sel.at[0], kv_in.at[2], kv_send.at[0], kv_recv.at[0], (place(2), m)),
        remote(kv_sel.at[1], kv_in.at[3], kv_send.at[1], kv_recv.at[1], (place(-2), m)),
        remote(kv_sel.at[0], kv_in.at[0], kv_send.at[2], kv_recv.at[2], (place(1), m)),
        remote(kv_sel.at[1], kv_in.at[1], kv_send.at[3], kv_recv.at[3], (place(-1), m)),
        remote(kv_sel.at[1], kv_other.at[0], kv_send.at[4], kv_recv.at[4], (place(1), m)),
        remote(kv_sel.at[0], kv_other.at[1], kv_send.at[5], kv_recv.at[5], (place(-1), m)),
    ]
    started += kv_copies
    tell(0)

    loads[5].wait()
    spread = jnp.broadcast_to(owners_ref[...], (n_blocks, n_blocks)).T
    slot_of = lax.broadcasted_iota(jnp.int32, (n_blocks, n_blocks), 1)
    block_of = lax.broadcasted_iota(jnp.int32, (n_blocks, n_blocks), 0)
    inv_v[...] = jnp.max(jnp.where(spread == slot_of, block_of, 0), 0, keepdims=True)
    inv_copy = pltpu.make_async_copy(inv_v, inv_s, load_sem.at[9])
    inv_copy.start()

    for load in loads[6:]:
        load.wait()
    xt_v[...] = x_v[...].T
    inv_copy.wait()

    heard(0)
    tell(1)
    for copy in kv_copies[:4]:
        copy.wait_recv()

    row = lax.broadcasted_iota(jnp.int32, (half, half), 0)
    col = lax.broadcasted_iota(jnp.int32, (half, half), 1)
    rs_copies = []
    for slot in range(2):
        if slot == 0:
            window = [kv_own[0], kv_in[jnp.where(up, 0, 1)], kv_in[jnp.where(up, 2, 3)]]
        else:
            for copy in kv_copies[4:]:
                copy.wait_recv()
            window = [
                kv_own[1],
                jnp.where(last, kv_own[0], kv_in[jnp.where(up, 1, 0)]),
                jnp.where(
                    second_last,
                    kv_other[jnp.where(up, 1, 0)],
                    kv_in[jnp.where(last, jnp.where(up, 0, 1), jnp.where(up, 3, 2))],
                ),
            ]
        keys = jnp.concatenate([pair[0] for pair in window], 0)
        values = jnp.concatenate([pair[1] for pair in window], 0)
        queries = q_ref[slot * half : (slot + 1) * half, :]
        grads = g_ref[slot * half : (slot + 1) * half, :]
        position = first if slot == 0 else 2 * n_seq - 1 - first
        visible = jnp.concatenate(
            [
                row - col >= 0,
                jnp.broadcast_to(position >= 1, (half, half)),
                (row - col < 0) & (position >= 2),
            ],
            1,
        )
        scores = jnp.where(visible, contract(queries, keys, ((1,), (1,))) * score_scale, MASKED)
        dprob = contract(grads, values, ((1,), (1,)))
        top = jnp.max(scores, -1, keepdims=True)
        raw = jnp.exp(scores - top)
        prob = raw * (1.0 / jnp.sum(raw, -1, keepdims=True))
        prob_b = prob.astype(BF16)
        delta = jnp.sum(prob_b.astype(F32) * dprob, -1, keepdims=True)
        dscore = (prob * (dprob - delta)).astype(BF16)
        value_grad = contract(prob_b, grads, ((0,), (0,)))
        key_grad = contract(dscore, queries, ((0,), (0,))) * score_scale
        qg_ref[slot * half : (slot + 1) * half, :] = (
            contract(dscore, keys, ((1,), (0,))) * score_scale
        ).astype(BF16)
        for part in range(3):
            here = slice(part * half, (part + 1) * half)
            terms_own[3 * slot + part, :, :hd] = key_grad[here]
            terms_own[3 * slot + part, :, hd:] = value_grad[here]
            terms[3 * slot + part, :, :hd] = key_grad[here].astype(BF16)
            terms[3 * slot + part, :, hd:] = value_grad[here].astype(BF16)

        if slot == 0:
            heard(1)
            for i in range(2, len(rounds)):
                tell(i)
        these = pl.ds(3 * slot, 3)
        rs_copies.append(
            [
                remote(
                    terms.at[these, pl.ds(pl.multiple_of(mate(offsets[i]) * cut, cut), cut), :],
                    terms_in.at[i, these],
                    rs_send.at[slot, i],
                    rs_recv.at[slot, i],
                    (s, mate(offsets[i])),
                )
                for i in range(n_mp - 1)
            ]
        )
        started += rs_copies[-1]
    my_rows = pl.ds(pl.multiple_of(m * cut, cut), cut)
    total = []
    for slot in range(2):
        part = terms_own[3 * slot : 3 * slot + 3, my_rows, :]
        for i in reversed(range(n_mp - 1)):
            rs_copies[slot][i].wait_recv()
            part = part + terms_in[i, 3 * slot : 3 * slot + 3].astype(F32)
        total += [part[0], part[1], part[2]]

    own0, down1, down2, own1, up1, up2 = total
    own0 = own0 + jnp.where(last, up1, 0.0)
    down1 = down1 + jnp.where(last, up2, 0.0)
    up1 = jnp.where(last, 0.0, up1)
    crossing = jnp.where(second_last, up2, 0.0)
    up2 = jnp.where(last | second_last, 0.0, up2)
    nothing = jnp.zeros_like(own0)
    pass_near[0, 0] = jnp.where(up, crossing, down1).astype(BF16)
    pass_near[0, 1] = jnp.where(up, up1, nothing).astype(BF16)
    pass_near[1, 0] = jnp.where(up, down1, crossing).astype(BF16)
    pass_near[1, 1] = jnp.where(up, nothing, up1).astype(BF16)
    pass_far[0] = jnp.where(up, up2, down2).astype(BF16)
    pass_far[1] = jnp.where(up, down2, up2).astype(BF16)
    pass_copies = [
        remote(pass_near.at[0], pass_near_in.at[0], pass_send.at[0], pass_recv.at[0], (place(1), m)),
        remote(pass_near.at[1], pass_near_in.at[1], pass_send.at[1], pass_recv.at[1], (place(-1), m)),
        remote(pass_far.at[0], pass_far_in.at[0], pass_send.at[2], pass_recv.at[2], (place(2), m)),
        remote(pass_far.at[1], pass_far_in.at[1], pass_send.at[3], pass_recv.at[3], (place(-2), m)),
    ]
    started += pass_copies
    for copy in pass_copies:
        copy.wait_recv()
    from_before = pass_far_in[0].astype(F32)
    from_after = pass_far_in[1].astype(F32)
    near = pass_near_in[0].astype(F32) + pass_near_in[1].astype(F32)
    own0 = own0 + near[0] + jnp.where(up, from_after, from_before)
    own1 = own1 + near[1] + jnp.where(up, from_before, from_after)
    fin[0] = own0.astype(BF16)
    fin[1] = own1.astype(BF16)
    kvg[:, my_rows, :] = fin[...]
    ag_copies = [
        remote(fin, kvg.at[:, my_rows, :], ag_send.at[i], ag_recv.at[i], (s, mate(offsets[i])))
        for i in range(n_mp - 1)
    ]
    started += ag_copies
    for copy in ag_copies:
        copy.wait_recv()

    kv_grad = kvg[...].reshape(rows, 2 * hd)
    lane = lax.broadcasted_iota(jnp.int32, (BLK // 2, 2 * BLK), 1)
    step = min(STEP, n_blocks // 4)
    for i in range(n_blocks // (4 * step)):
        part = contract(xt_v[i * step * BLK : (i + 1) * step * BLK, :], kv_grad, ((1,), (0,)))
        for r in range(step):
            for j in range(2):
                tile = part[r * BLK : (r + 1) * BLK, j * 2 * BLK : (j + 1) * 2 * BLK]
                upper, lower = tile[: BLK // 2], tile[BLK // 2 :]
                pieces[(i * step + r) * 4 + 2 * j] = jnp.where(
                    lane < BLK, upper, pltpu.roll(lower, BLK, 1)
                )
                pieces[(i * step + r) * 4 + 2 * j + 1] = jnp.where(
                    lane < BLK, pltpu.roll(upper, BLK, 1), lower
                )

    def owner_piece(p, whose_y, whose_core):
        t = n_z // 2 + (p + 1) // 2 * (1 - 2 * lax.rem(p, 2))
        slot = 2 * (2 * lax.rem(z + t, n_z) + whose_y) + whose_core
        return pieces[inv_s[0, slot] & (n_blocks - 1)]

    n_parts = min(PARTS, n_z // 2)
    part = n_z // n_parts
    core_copies = []
    for k, whose_y in enumerate((1 - y, y)):
        for c in range(n_parts):

            @pl.loop(c * part, (c + 1) * part, unroll=True)
            def _(p, k=k, whose_y=whose_y):
                core_out[k, p] = owner_piece(p, whose_y, 1 - core).astype(BF16)

            here = pl.ds(c * part, part)
            core_copies.append(
                remote(
                    core_out.at[k, here],
                    core_in.at[k, here],
                    core_send.at[k, c],
                    core_recv.at[k, c],
                    (s + 1 - 2 * core, m),
                )
            )
    for k, whose_y in enumerate((1 - y, y)):

        @pl.loop(0, n_z, unroll=True)
        def _(p, k=k, whose_y=whose_y):
            keep[k, p] = owner_piece(p, whose_y, core)

    y_copies = []
    for c in range(n_parts):
        here = pl.ds(c * part, part)
        core_copies[c].wait_recv()
        y_out[here] = (keep[0, here] + core_in[0, here].astype(F32)).astype(BF16)
        y_copies.append(
            remote(y_out.at[here], y_in.at[here], y_send.at[c], y_recv.at[c], (s + 2 - 4 * y, m))
        )
    for i in range(2, len(rounds)):
        heard(i)
    for copy in started + core_copies:
        copy.wait_send()
    for copy in core_copies[n_parts:]:
        copy.wait_recv()
    z_copies = []
    for c in range(n_parts):
        here = pl.ds(c * part, part)
        ours = keep[1, here] + core_in[1, here].astype(F32)
        y_copies[c].wait_recv()
        ours = ours + y_in[here].astype(F32)
        z_out[here] = ours.astype(BF16)
        for p in range(c * part, min((c + 1) * part, n_z - 1)):
            t = n_z // 2 + (p + 1) // 2 * (1 - 2 * (p % 2))
            z_copies.append(
                remote(z_out.at[p], z_in.at[p], z_send.at[p], z_recv.at[p], (place(4 * t), m))
            )
    for copy in y_copies:
        copy.wait_send()
    owned = ours[part - 1]
    for p in reversed(range(n_z - 1)):
        z_copies[p].wait_recv()
        owned = owned + z_in[p].astype(F32)
    sum_ref[...] = owned
    for copy in z_copies:
        copy.wait_send()


def finish(weight_scale, qg_ref, sum_ref, qg_out, block_out, left_out, right_out):
    qg_out[...] = qg_ref[...]
    owned = sum_ref[...] * weight_scale
    block = jnp.concatenate([owned[:, :BLK], owned[:, BLK:]], 0)
    block_out[0, 0] = block

    def exact(dims):
        return (
            lax.dot_general(
                block,
                block,
                (dims, ((), ())),
                precision=lax.Precision.HIGHEST,
                preferred_element_type=F32,
            )
            / BLK
        )

    left_out[0, 0] = exact(((1,), (1,)))
    right_out[0, 0] = exact(((0,), (0,)))


def shards(n_seq, n_mp, layer_input, query_heads, key_head, value_head, attn_grad, block_order, owners):
    rows, columns = layer_input.shape
    half = rows // 2
    hd = key_head.shape[1]
    cut = half // n_mp
    n_z = n_seq // 4
    n_blocks = owners.shape[1]
    shape = (BLK // 2, 2 * BLK)
    vmem = pl.BlockSpec(memory_space=pltpu.VMEM)
    stat = jax.ShapeDtypeStruct((1, 1, BLK, BLK), F32)
    dma = pltpu.SemaphoreType.DMA
    query_part = jax.ShapeDtypeStruct((rows, hd), BF16)
    query_grad, owned = pl.pallas_call(
        functools.partial(kernel, n_seq, n_mp),
        out_shape=(query_part, jax.ShapeDtypeStruct(shape, F32)),
        in_specs=[pl.BlockSpec(memory_space=pl.ANY)] * 7,
        out_specs=(vmem, vmem),
        scratch_shapes=[
            pltpu.SMEM((2 * n_seq,), jnp.int32),
            pltpu.VMEM((1, n_blocks), jnp.int32),
            pltpu.VMEM((rows, hd), BF16),
            pltpu.VMEM((rows, hd), BF16),
            pltpu.VMEM((rows, columns), BF16),
            pltpu.VMEM((columns, rows), BF16),
            pltpu.VMEM((1, n_blocks), jnp.int32),
            pltpu.SMEM((1, n_blocks), jnp.int32),
            pltpu.VMEM((2, 2, half, hd), BF16),
            pltpu.VMEM((2, 2, half, hd), BF16),
            pltpu.VMEM((4, 2, half, hd), BF16),
            pltpu.VMEM((2, 2, half, hd), BF16),
            pltpu.VMEM((6, half, 2 * hd), BF16),
            pltpu.VMEM((6, half, 2 * hd), F32),
            pltpu.VMEM((n_mp - 1, 6, cut, 2 * hd), BF16),
            pltpu.VMEM((2, 2, cut, 2 * hd), BF16),
            pltpu.VMEM((2, cut, 2 * hd), BF16),
            pltpu.VMEM((2, 2, cut, 2 * hd), BF16),
            pltpu.VMEM((2, cut, 2 * hd), BF16),
            pltpu.VMEM((2, cut, 2 * hd), BF16),
            pltpu.VMEM((2, half, 2 * hd), BF16),
            pltpu.VMEM((n_blocks, *shape), F32),
            pltpu.VMEM((2, n_z, *shape), F32),
            pltpu.VMEM((2, n_z, *shape), BF16),
            pltpu.VMEM((2, n_z, *shape), BF16),
            pltpu.VMEM((n_z, *shape), BF16),
            pltpu.VMEM((n_z, *shape), BF16),
            pltpu.VMEM((n_z, *shape), BF16),
            pltpu.VMEM((n_z - 1, *shape), BF16),
            dma((10,)),
            pltpu.SemaphoreType.REGULAR((4,)),
            dma((6,)),
            dma((6,)),
            dma((2, n_mp - 1)),
            dma((2, n_mp - 1)),
            dma((4,)),
            dma((4,)),
            dma((n_mp - 1,)),
            dma((n_mp - 1,)),
            dma((2, PARTS)),
            dma((2, PARTS)),
            dma((PARTS,)),
            dma((PARTS,)),
            dma((n_z - 1,)),
            dma((n_z - 1,)),
        ],
        compiler_params=pltpu.CompilerParams(
            collective_id=0, has_side_effects=True, vmem_limit_bytes=60 * 1024 * 1024
        ),
    )(block_order, owners, layer_input, query_heads, key_head, value_head, attn_grad)
    return pl.pallas_call(
        functools.partial(finish, 1.0 / math.sqrt(rows * n_seq)),
        out_shape=(query_part, stat, stat, stat),
        in_specs=[vmem, vmem],
        out_specs=(vmem, vmem, vmem, vmem),
        compiler_params=pltpu.CompilerParams(vmem_limit_bytes=60 * 1024 * 1024),
    )(query_grad, owned)


def solution(mesh):
    return jax.shard_map(
        functools.partial(shards, mesh.shape["seq"], mesh.shape["mp"]),
        mesh=mesh,
        in_specs=(
            P("seq", "mp"),
            P("seq", "mp"),
            P("seq", None),
            P("seq", None),
            P("seq", "mp"),
            P(),
            P("mp", None),
        ),
        out_specs=(
            P("seq", "mp"),
            P("mp", "seq", None, None),
            P("mp", "seq", None, None),
            P("mp", "seq", None, None),
        ),
        check_vma=False,
    )
```

```python
import functools
import math

import jax
import jax.numpy as jnp
from jax import lax
from jax.experimental import pallas as pl
from jax.experimental.pallas import tpu as pltpu
from jax.sharding import PartitionSpec as P

BLK = 64
STEP = 4
PARTS = 4
MASKED = -1e30
MESH = pl.DeviceIdType.MESH
F32 = jnp.float32
BF16 = jnp.bfloat16


def contract(a, b, dims):
    return lax.dot_general(a, b, (dims, ((), ())), preferred_element_type=F32)


def kernel(
    n_seq,
    n_mp,
    order_hbm,
    owners_hbm,
    x_hbm,
    q_hbm,
    k_hbm,
    v_hbm,
    g_hbm,
    qg_hbm,
    sum_ref,
    qg_ref,
    order_ref,
    owners_ref,
    q_ref,
    g_ref,
    x_v,
    xt_v,
    inv_v,
    inv_s,
    k_own,
    k_sel,
    k_in,
    k_other,
    v_own,
    v_sel,
    v_in,
    v_other,
    terms_k,
    terms_v,
    terms_k_in,
    terms_v_in,
    pass_near,
    pass_far,
    pass_near_in,
    pass_far_in,
    own_out,
    own_in,
    kept,
    fin,
    kvg,
    pieces,
    keep,
    far_out,
    far_in,
    core_out,
    core_in,
    y_out,
    y_in,
    z_out,
    z_in,
    load_sem,
    word_sem,
    kv_send,
    kv_recv,
    rs_send,
    rs_recv,
    pass_send,
    pass_recv,
    ag_send,
    ag_recv,
    far_send,
    far_recv,
    core_send,
    core_recv,
    y_send,
    y_recv,
    z_send,
    z_recv,
):
    n_z = n_seq // 4
    rows = q_ref.shape[0]
    half = rows // 2
    hd = q_ref.shape[1]
    n_x = min(4, n_mp)
    n_y = n_mp // n_x
    cut = half // n_x
    n_blocks = pieces.shape[0]
    score_scale = 1.0 / math.sqrt(hd)

    s = lax.axis_index("seq")
    m = lax.axis_index("mp")
    core = lax.rem(s, 2)
    y = lax.rem(s // 2, 2)
    z = s // 4

    def place(distance):
        return lax.rem(s + distance + n_seq, n_seq)

    def mate(a, b):
        return lax.rem(m // n_x + a, n_y) * n_x + lax.rem(lax.rem(m, n_x) + b, n_x)

    along_x = sorted(range(1, n_x), key=lambda b: -min(b, n_x - b))

    barrier = pltpu.get_barrier_semaphore()
    next_z = [(place(4 * t), m) for t in sorted({1, n_z - 1})]
    crossing = {2: y, -2: 1 - y, 1: core * y, -1: (1 - core) * (1 - y)}
    beside = {d: (place(d), lax.rem(m + cross * n_x, n_mp)) for d, cross in crossing.items()}
    partners = list(beside.values()) + next_z
    partners += [(s, mate(0, b)) for b in along_x] + [(s, mate(a, 0)) for a in range(1, n_y)]
    reaches = [1 << i for i in range((n_z // 2).bit_length() - 1)]
    along_z = [[(place(4 * t), m) for t in (r, n_z - r)] for r in reaches[1:]]
    rounds = [partners, *along_z]

    def tell(i):
        for partner in rounds[i]:
            pl.semaphore_signal(
                word_sem.at[i], inc=1, device_id=partner, device_id_type=MESH
            )

    def heard(i):
        pl.semaphore_wait(word_sem.at[i], len(rounds[i]))

    for partner in partners:
        pl.semaphore_signal(barrier, inc=1, device_id=partner, device_id_type=MESH)

    loads = [
        pltpu.make_async_copy(src, dst, load_sem.at[i])
        for i, (src, dst) in enumerate(
            [
                (order_hbm, order_ref),
                (k_hbm.at[0:half], k_own.at[0]),
                (v_hbm.at[0:half], v_own.at[0]),
                (k_hbm.at[half:rows], k_own.at[1]),
                (v_hbm.at[half:rows], v_own.at[1]),
                (owners_hbm, owners_ref),
                (q_hbm, q_ref),
                (g_hbm, g_ref),
                (x_hbm, x_v),
            ]
        )
    ]
    for load in loads:
        load.start()

    for load in loads[:5]:
        load.wait()

    first = order_ref[2 * s]
    following = order_ref[2 * place(1)]
    up = ((following - first + n_seq) & (n_seq - 1)) == 1
    last = first == n_seq - 1
    second_last = first == n_seq - 2

    for own, sel in ((k_own, k_sel), (v_own, v_sel)):
        sel[0] = own[jnp.where(up, 0, 1)]
        sel[1] = own[jnp.where(up, 1, 0)]

    pl.semaphore_wait(barrier, len(partners))

    def remote(src, dst, send_sem, recv_sem, to):
        copy = pltpu.make_async_remote_copy(
            src_ref=src,
            dst_ref=dst,
            send_sem=send_sem,
            recv_sem=recv_sem,
            device_id=to,
            device_id_type=MESH,
        )
        copy.start()
        return copy

    started = []
    def spread_window(j, sel, near_far, other):
        pieces_of = [
            (sel.at[0], near_far.at[2], beside[2]),
            (sel.at[1], near_far.at[3], beside[-2]),
            (sel.at[0], near_far.at[0], beside[1]),
            (sel.at[1], near_far.at[1], beside[-1]),
            (sel.at[1], other.at[0], beside[1]),
            (sel.at[0], other.at[1], beside[-1]),
        ]
        return [
            remote(src, dst, kv_send.at[j, i], kv_recv.at[j, i], to)
            for i, (src, dst, to) in enumerate(pieces_of)
        ]

    k_copies = spread_window(0, k_sel, k_in, k_other)
    v_copies = spread_window(1, v_sel, v_in, v_other)
    started += k_copies + v_copies
    tell(0)

    loads[5].wait()
    spread = jnp.broadcast_to(owners_ref[...], (n_blocks, n_blocks)).T
    slot_of = lax.broadcasted_iota(jnp.int32, (n_blocks, n_blocks), 1)
    block_of = lax.broadcasted_iota(jnp.int32, (n_blocks, n_blocks), 0)
    inv_v[...] = jnp.max(jnp.where(spread == slot_of, block_of, 0), 0, keepdims=True)
    inv_copy = pltpu.make_async_copy(inv_v, inv_s, load_sem.at[9])
    inv_copy.start()

    for load in loads[6:]:
        load.wait()
    xt_v[...] = x_v[...].T
    inv_copy.wait()

    row = lax.broadcasted_iota(jnp.int32, (half, half), 0)
    col = lax.broadcasted_iota(jnp.int32, (half, half), 1)
    queries = [q_ref[slot * half : (slot + 1) * half, :] for slot in range(2)]
    grads = [g_ref[slot * half : (slot + 1) * half, :] for slot in range(2)]
    by_row = ((1,), (1,))
    scores_own = [contract(queries[slot], k_own[slot], by_row) for slot in range(2)]
    dprob_own = [contract(grads[slot], v_own[slot], by_row) for slot in range(2)]

    def before(slot, own, near_far, other):
        if slot == 0:
            blocks = [near_far[jnp.where(up, 0, 1)], near_far[jnp.where(up, 2, 3)]]
        else:
            blocks = [
                jnp.where(last, own[0], near_far[jnp.where(up, 1, 0)]),
                jnp.where(
                    second_last,
                    other[jnp.where(up, 1, 0)],
                    near_far[jnp.where(last, jnp.where(up, 0, 1), jnp.where(up, 3, 2))],
                ),
            ]
        return jnp.concatenate(blocks, 0)

    def send_terms(j, terms, terms_in):
        copies = [
            remote(
                terms.at[:, pl.ds(pl.multiple_of(lax.rem(mate(0, b), n_x) * cut, cut), cut), :],
                terms_in.at[i],
                rs_send.at[j, i],
                rs_recv.at[j, i],
                (s, mate(0, b)),
            )
            for i, b in enumerate(along_x)
        ]
        started.extend(copies)
        return copies

    heard(0)
    for i in range(1, min(2, len(rounds))):
        tell(i)
    for copy in k_copies:
        copy.wait_recv()
    windows = [before(slot, k_own, k_in, k_other) for slot in range(2)]
    probs = []
    probs_b = []
    for slot in range(2):
        position = first if slot == 0 else 2 * n_seq - 1 - first
        visible = jnp.concatenate(
            [
                row - col >= 0,
                jnp.broadcast_to(position >= 1, (half, half)),
                (row - col < 0) & (position >= 2),
            ],
            1,
        )
        scores = jnp.concatenate(
            [scores_own[slot], contract(queries[slot], windows[slot], by_row)], 1
        )
        scores = jnp.where(visible, scores * score_scale, MASKED)
        top = jnp.max(scores, -1, keepdims=True)
        raw = jnp.exp(scores - top)
        probs.append(raw * (1.0 / jnp.sum(raw, -1, keepdims=True)))
        probs_b.append(probs[slot].astype(BF16))
        value_grad = contract(probs_b[slot], grads[slot], ((0,), (0,))).astype(BF16)
        terms_v[3 * slot : 3 * slot + 3] = value_grad.reshape(3, half, hd)
    rs_v_copies = send_terms(0, terms_v, terms_v_in)

    for copy in v_copies:
        copy.wait_recv()
    dscores = []
    for slot in range(2):
        values = before(slot, v_own, v_in, v_other)
        dprob = jnp.concatenate([dprob_own[slot], contract(grads[slot], values, by_row)], 1)
        delta = jnp.sum(probs_b[slot].astype(F32) * dprob, -1, keepdims=True)
        dscores.append((probs[slot] * (dprob - delta)).astype(BF16))
        key_grad = contract(dscores[slot], queries[slot], ((0,), (0,))).astype(BF16)
        terms_k[3 * slot : 3 * slot + 3] = key_grad.reshape(3, half, hd)
    rs_k_copies = send_terms(1, terms_k, terms_k_in)

    for i in range(1, min(2, len(rounds))):
        heard(i)
    for i in range(2, len(rounds)):
        tell(i)
    for slot in range(2):
        query_grad = contract(dscores[slot][:, :half], k_own[slot], ((1,), (0,)))
        query_grad += contract(dscores[slot][:, half:], windows[slot], ((1,), (0,)))
        qg_ref[slot * half : (slot + 1) * half, :] = (query_grad * score_scale).astype(BF16)
    qg_copy = pltpu.make_async_copy(qg_ref, qg_hbm, load_sem.at[10])
    qg_copy.start()

    my_rows = pl.ds(pl.multiple_of(lax.rem(m, n_x) * cut, cut), cut)

    def head_sum(copies, terms, terms_in):
        total = terms[:, my_rows, :].astype(F32)
        for i in reversed(range(n_x - 1)):
            copies[i].wait_recv()
            total = total + terms_in[i].astype(F32)
        return total

    def give_back(j, total):
        own0, down1, down2, own1, up1, up2 = [total[i] for i in range(6)]
        own0 = own0 + jnp.where(last, up1, 0.0)
        down1 = down1 + jnp.where(last, up2, 0.0)
        up1 = jnp.where(last, 0.0, up1)
        across = jnp.where(second_last, up2, 0.0)
        up2 = jnp.where(last | second_last, 0.0, up2)
        nothing = jnp.zeros_like(own0)
        pass_near[j, 0, 0] = jnp.where(up, across, down1).astype(BF16)
        pass_near[j, 0, 1] = jnp.where(up, up1, nothing).astype(BF16)
        pass_near[j, 1, 0] = jnp.where(up, down1, across).astype(BF16)
        pass_near[j, 1, 1] = jnp.where(up, nothing, up1).astype(BF16)
        pass_far[j, 0] = jnp.where(up, up2, down2).astype(BF16)
        pass_far[j, 1] = jnp.where(up, down2, up2).astype(BF16)
        kept[j, 0] = own0
        kept[j, 1] = own1
        own_out[j] = kept[j].astype(BF16)
        returns = [
            (pass_far.at[j, 0], pass_far_in.at[j, 0], place(2), 0),
            (pass_far.at[j, 1], pass_far_in.at[j, 1], place(-2), 1),
            (pass_near.at[j, 0], pass_near_in.at[j, 0], place(1), 2),
            (pass_near.at[j, 1], pass_near_in.at[j, 1], place(-1), 3),
            (own_out.at[j], own_in.at[j], s, 4),
        ]
        copies = [
            remote(src, dst.at[a], pass_send.at[j, i, a], pass_recv.at[j, i, a], (to, mate(a, 0)))
            for a in reversed(range(n_y))
            for src, dst, to, i in returns
            if a > 0 or i < 4
        ]
        started.extend(copies)
        return copies

    def gather(j, copies):
        for copy in copies:
            copy.wait_recv()
        total = kept[j]
        far_before = far_after = 0.0
        for a in range(n_y):
            total = total + pass_near_in[j, 0, a].astype(F32) + pass_near_in[j, 1, a].astype(F32)
            far_before = far_before + pass_far_in[j, 0, a].astype(F32)
            far_after = far_after + pass_far_in[j, 1, a].astype(F32)
            if a > 0:
                total = total + own_in[j, a].astype(F32)
        fin[j, 0] = (total[0] + jnp.where(up, far_after, far_before)).astype(BF16)
        fin[j, 1] = (total[1] + jnp.where(up, far_before, far_after)).astype(BF16)
        kvg[j, :, my_rows, :] = fin[j]
        copies = [
            remote(
                fin.at[j],
                kvg.at[j, :, my_rows, :],
                ag_send.at[j, i],
                ag_recv.at[j, i],
                (s, mate(0, b)),
            )
            for i, b in enumerate(along_x)
        ]
        started.extend(copies)
        return copies

    total_v = head_sum(rs_v_copies, terms_v, terms_v_in)
    pass_v_copies = give_back(1, total_v)
    total_k = head_sum(rs_k_copies, terms_k, terms_k_in) * score_scale
    pass_k_copies = give_back(0, total_k)
    ag_v_copies = gather(1, pass_v_copies)
    ag_k_copies = gather(0, pass_k_copies)

    lane = lax.broadcasted_iota(jnp.int32, (BLK // 2, 2 * BLK), 1)
    step = min(STEP, n_blocks // 4)
    for j, copies in ((1, ag_v_copies), (0, ag_k_copies)):
        for copy in copies:
            copy.wait_recv()
        kv_grad = kvg[j].reshape(rows, hd)
        for i in range(n_blocks // (4 * step)):
            part = contract(xt_v[i * step * BLK : (i + 1) * step * BLK, :], kv_grad, ((1,), (0,)))
            for r in range(step):
                tile = part[r * BLK : (r + 1) * BLK]
                upper, lower = tile[: BLK // 2], tile[BLK // 2 :]
                block = (i * step + r) * 4 + 2 * j
                pieces[block] = jnp.where(lane < BLK, upper, pltpu.roll(lower, BLK, 1))
                pieces[block + 1] = jnp.where(lane < BLK, pltpu.roll(upper, BLK, 1), lower)

    def owner_piece(p, whose_y, whose_core):
        t = n_z // 2 + (p + 1) // 2 * (1 - 2 * (p % 2))
        slot = 2 * (2 * lax.rem(z + t, n_z) + whose_y) + whose_core
        return pieces[inv_s[0, slot] & (n_blocks - 1)]

    n_parts = min(PARTS, n_z // 2)
    part = n_z // n_parts
    far_copies = []
    for g, (dy, dc) in enumerate([(1, 1), (1, 0), (0, 1)]):
        to_y, to_core = lax.rem(y + dy, 2), lax.rem(core + dc, 2)
        for p in range(part):
            far_out[g, p] = owner_piece(p, to_y, to_core).astype(BF16)
        far_copies.append(
            remote(
                far_out.at[g],
                far_in.at[g],
                far_send.at[g],
                far_recv.at[g],
                (4 * z + 2 * to_y + to_core, m),
            )
        )
    core_copies = {}
    for k, whose_y in enumerate((1 - y, y)):
        for c in range(1, n_parts):
            for p in range(c * part, (c + 1) * part):
                core_out[k, p] = owner_piece(p, whose_y, 1 - core).astype(BF16)
            here = pl.ds(c * part, part)
            core_copies[k, c] = remote(
                core_out.at[k, here],
                core_in.at[k, here],
                core_send.at[k, c],
                core_recv.at[k, c],
                (s + 1 - 2 * core, m),
            )
    for p in range(part, n_z):
        keep[0, p] = owner_piece(p, 1 - y, core)
    for p in range(n_z):
        keep[1, p] = owner_piece(p, y, core)

    y_copies = {}
    for c in range(1, n_parts):
        here = pl.ds(c * part, part)
        core_copies[0, c].wait_recv()
        y_out[here] = (keep[0, here] + core_in[0, here].astype(F32)).astype(BF16)
        y_copies[c] = remote(
            y_out.at[here], y_in.at[here], y_send.at[c], y_recv.at[c], (s + 2 - 4 * y, m)
        )
    for i in range(2, len(rounds)):
        heard(i)
    z_copies = []
    for c in range(n_parts):
        here = pl.ds(c * part, part)
        ours = keep[1, here]
        if c == 0:
            for g in (2, 1, 0):
                far_copies[g].wait_recv()
                ours = ours + far_in[g].astype(F32)
        else:
            core_copies[1, c].wait_recv()
            ours = ours + core_in[1, here].astype(F32)
            y_copies[c].wait_recv()
            ours = ours + y_in[here].astype(F32)
        z_out[here] = ours.astype(BF16)
        for p in range(c * part, min((c + 1) * part, n_z - 1)):
            t = n_z // 2 + (p + 1) // 2 * (1 - 2 * (p % 2))
            z_copies.append(
                remote(z_out.at[p], z_in.at[p], z_send.at[p], z_recv.at[p], (place(4 * t), m))
            )
    for copy in [*started, *far_copies, *core_copies.values(), *y_copies.values()]:
        copy.wait_send()
    qg_copy.wait()
    owned = ours[part - 1]
    for p in reversed(range(n_z - 1)):
        z_copies[p].wait_recv()
        owned = owned + z_in[p].astype(F32)
    sum_ref[...] = owned
    for copy in z_copies:
        copy.wait_send()


def finish(weight_scale, qg_ref, sum_ref, qg_out, block_out, left_out, right_out):
    qg_out[...] = qg_ref[...]
    owned = sum_ref[...] * weight_scale
    block = jnp.concatenate([owned[:, :BLK], owned[:, BLK:]], 0)
    block_out[0, 0] = block

    def exact(dims):
        return (
            lax.dot_general(
                block,
                block,
                (dims, ((), ())),
                precision=lax.Precision.HIGHEST,
                preferred_element_type=F32,
            )
            / BLK
        )

    left_out[0, 0] = exact(((1,), (1,)))
    right_out[0, 0] = exact(((0,), (0,)))


def shards(n_seq, n_mp, layer_input, query_heads, key_head, value_head, attn_grad, block_order, owners):
    rows, columns = layer_input.shape
    half = rows // 2
    hd = key_head.shape[1]
    n_x = min(4, n_mp)
    n_y = n_mp // n_x
    cut = half // n_x
    n_z = n_seq // 4
    n_blocks = owners.shape[1]
    shape = (BLK // 2, 2 * BLK)
    vmem = pl.BlockSpec(memory_space=pltpu.VMEM)
    stat = jax.ShapeDtypeStruct((1, 1, BLK, BLK), F32)
    dma = pltpu.SemaphoreType.DMA
    query_part = jax.ShapeDtypeStruct((rows, hd), BF16)
    query_grad, owned = pl.pallas_call(
        functools.partial(kernel, n_seq, n_mp),
        out_shape=(query_part, jax.ShapeDtypeStruct(shape, F32)),
        in_specs=[pl.BlockSpec(memory_space=pl.ANY)] * 7,
        out_specs=(pl.BlockSpec(memory_space=pl.ANY), vmem),
        scratch_shapes=[
            pltpu.VMEM((rows, hd), BF16),
            pltpu.SMEM((2 * n_seq,), jnp.int32),
            pltpu.VMEM((1, n_blocks), jnp.int32),
            pltpu.VMEM((rows, hd), BF16),
            pltpu.VMEM((rows, hd), BF16),
            pltpu.VMEM((rows, columns), BF16),
            pltpu.VMEM((columns, rows), BF16),
            pltpu.VMEM((1, n_blocks), jnp.int32),
            pltpu.SMEM((1, n_blocks), jnp.int32),
            pltpu.VMEM((2, half, hd), BF16),
            pltpu.VMEM((2, half, hd), BF16),
            pltpu.VMEM((4, half, hd), BF16),
            pltpu.VMEM((2, half, hd), BF16),
            pltpu.VMEM((2, half, hd), BF16),
            pltpu.VMEM((2, half, hd), BF16),
            pltpu.VMEM((4, half, hd), BF16),
            pltpu.VMEM((2, half, hd), BF16),
            pltpu.VMEM((6, half, hd), BF16),
            pltpu.VMEM((6, half, hd), BF16),
            pltpu.VMEM((n_x - 1, 6, cut, hd), BF16),
            pltpu.VMEM((n_x - 1, 6, cut, hd), BF16),
            pltpu.VMEM((2, 2, 2, cut, hd), BF16),
            pltpu.VMEM((2, 2, cut, hd), BF16),
            pltpu.VMEM((2, 2, n_y, 2, cut, hd), BF16),
            pltpu.VMEM((2, 2, n_y, cut, hd), BF16),
            pltpu.VMEM((2, 2, cut, hd), BF16),
            pltpu.VMEM((2, n_y, 2, cut, hd), BF16),
            pltpu.VMEM((2, 2, cut, hd), F32),
            pltpu.VMEM((2, 2, cut, hd), BF16),
            pltpu.VMEM((2, 2, half, hd), BF16),
            pltpu.VMEM((n_blocks, *shape), F32),
            pltpu.VMEM((2, n_z, *shape), F32),
            pltpu.VMEM((3, n_z // min(PARTS, n_z // 2), *shape), BF16),
            pltpu.VMEM((3, n_z // min(PARTS, n_z // 2), *shape), BF16),
            pltpu.VMEM((2, n_z, *shape), BF16),
            pltpu.VMEM((2, n_z, *shape), BF16),
            pltpu.VMEM((n_z, *shape), BF16),
            pltpu.VMEM((n_z, *shape), BF16),
            pltpu.VMEM((n_z, *shape), BF16),
            pltpu.VMEM((n_z - 1, *shape), BF16),
            dma((11,)),
            pltpu.SemaphoreType.REGULAR((4,)),
            dma((2, 6)),
            dma((2, 6)),
            dma((2, n_x - 1)),
            dma((2, n_x - 1)),
            dma((2, 5, n_y)),
            dma((2, 5, n_y)),
            dma((2, n_x - 1)),
            dma((2, n_x - 1)),
            dma((3,)),
            dma((3,)),
            dma((2, PARTS)),
            dma((2, PARTS)),
            dma((PARTS,)),
            dma((PARTS,)),
            dma((n_z - 1,)),
            dma((n_z - 1,)),
        ],
        compiler_params=pltpu.CompilerParams(
            collective_id=0, has_side_effects=True, vmem_limit_bytes=60 * 1024 * 1024
        ),
    )(block_order, owners, layer_input, query_heads, key_head, value_head, attn_grad)
    return pl.pallas_call(
        functools.partial(finish, 1.0 / math.sqrt(rows * n_seq)),
        out_shape=(query_part, stat, stat, stat),
        in_specs=[vmem, vmem],
        out_specs=(vmem, vmem, vmem, vmem),
        compiler_params=pltpu.CompilerParams(vmem_limit_bytes=60 * 1024 * 1024),
    )(query_grad, owned)


def solution(mesh):
    return jax.shard_map(
        functools.partial(shards, mesh.shape["seq"], mesh.shape["mp"]),
        mesh=mesh,
        in_specs=(
            P("seq", "mp"),
            P("seq", "mp"),
            P("seq", None),
            P("seq", None),
            P("seq", "mp"),
            P(),
            P("mp", None),
        ),
        out_specs=(
            P("seq", "mp"),
            P("mp", "seq", None, None),
            P("mp", "seq", None, None),
            P("mp", "seq", None, None),
        ),
        check_vma=False,
    )
```

```python
import functools
import math

import jax
import jax.numpy as jnp
from jax import lax
from jax.experimental import pallas as pl
from jax.experimental.pallas import tpu as pltpu
from jax.sharding import PartitionSpec as P

BLK = 64
STEP = 4
PARTS = 4
MASKED = -1e30
MESH = pl.DeviceIdType.MESH
F32 = jnp.float32
BF16 = jnp.bfloat16


def contract(a, b, dims):
    return lax.dot_general(a, b, (dims, ((), ())), preferred_element_type=F32)


def kernel(
    n_seq,
    n_mp,
    order_hbm,
    owners_hbm,
    x_hbm,
    q_hbm,
    k_hbm,
    v_hbm,
    g_hbm,
    qg_hbm,
    sum_ref,
    qg_ref,
    order_ref,
    owners_ref,
    q_ref,
    g_ref,
    x_v,
    xt_v,
    inv_v,
    inv_s,
    k_own,
    k_sel,
    k_in,
    k_other,
    v_own,
    v_sel,
    v_in,
    v_other,
    terms_k,
    terms_v,
    terms_k_in,
    terms_v_in,
    pass_near,
    pass_far,
    pass_near_in,
    pass_far_in,
    own_out,
    own_in,
    kept,
    fin,
    kvg,
    pieces,
    keep,
    far_out,
    far_in,
    core_out,
    core_in,
    y_out,
    y_in,
    z_out,
    z_in,
    load_sem,
    word_sem,
    kv_send,
    kv_recv,
    rs_send,
    rs_recv,
    pass_send,
    pass_recv,
    ag_send,
    ag_recv,
    far_send,
    far_recv,
    core_send,
    core_recv,
    y_send,
    y_recv,
    z_send,
    z_recv,
):
    n_z = n_seq // 4
    rows = q_ref.shape[0]
    half = rows // 2
    hd = q_ref.shape[1]
    n_x = min(4, n_mp)
    n_y = n_mp // n_x
    cut = half // n_x
    n_blocks = pieces.shape[0]
    score_scale = 1.0 / math.sqrt(hd)

    s = lax.axis_index("seq")
    m = lax.axis_index("mp")
    core = lax.rem(s, 2)
    y = lax.rem(s // 2, 2)
    z = s // 4

    def place(distance):
        return lax.rem(s + distance + n_seq, n_seq)

    def mate(a, b):
        return lax.rem(m // n_x + a, n_y) * n_x + lax.rem(lax.rem(m, n_x) + b, n_x)

    along_x = sorted(range(1, n_x), key=lambda b: -min(b, n_x - b))

    barrier = pltpu.get_barrier_semaphore()
    next_z = [(place(4 * t), m) for t in sorted({1, n_z - 1})]
    crossing = {2: y, -2: 1 - y, 1: core * y, -1: (1 - core) * (1 - y)}
    beside = {d: (place(d), lax.rem(m + cross * n_x, n_mp)) for d, cross in crossing.items()}
    partners = list(beside.values()) + next_z
    partners += [(s, mate(0, b)) for b in along_x] + [(s, mate(a, 0)) for a in range(1, n_y)]
    reaches = [1 << i for i in range((n_z // 2).bit_length() - 1)]
    along_z = [[(place(4 * t), m) for t in (r, n_z - r)] for r in reaches[1:]]
    rounds = [partners, *along_z]

    def tell(i):
        for partner in rounds[i]:
            pl.semaphore_signal(
                word_sem.at[i], inc=1, device_id=partner, device_id_type=MESH
            )

    def heard(i):
        pl.semaphore_wait(word_sem.at[i], len(rounds[i]))

    for partner in partners:
        pl.semaphore_signal(barrier, inc=1, device_id=partner, device_id_type=MESH)

    loads = [
        pltpu.make_async_copy(src, dst, load_sem.at[i])
        for i, (src, dst) in enumerate(
            [
                (order_hbm, order_ref),
                (k_hbm.at[0:half], k_own.at[0]),
                (v_hbm.at[0:half], v_own.at[0]),
                (k_hbm.at[half:rows], k_own.at[1]),
                (v_hbm.at[half:rows], v_own.at[1]),
                (owners_hbm, owners_ref),
                (q_hbm, q_ref),
                (g_hbm, g_ref),
                (x_hbm, x_v),
            ]
        )
    ]
    for load in loads:
        load.start()

    for load in loads[:5]:
        load.wait()

    first = order_ref[2 * s]
    following = order_ref[2 * place(1)]
    up = ((following - first + n_seq) & (n_seq - 1)) == 1
    last = first == n_seq - 1
    second_last = first == n_seq - 2

    for own, sel in ((k_own, k_sel), (v_own, v_sel)):
        sel[0] = own[jnp.where(up, 0, 1)]
        sel[1] = own[jnp.where(up, 1, 0)]

    pl.semaphore_wait(barrier, len(partners))

    def remote(src, dst, send_sem, recv_sem, to):
        copy = pltpu.make_async_remote_copy(
            src_ref=src,
            dst_ref=dst,
            send_sem=send_sem,
            recv_sem=recv_sem,
            device_id=to,
            device_id_type=MESH,
        )
        copy.start()
        return copy

    started = []
    def spread_window(j, sel, near_far, other):
        pieces_of = [
            (sel.at[0], near_far.at[2], beside[2]),
            (sel.at[1], near_far.at[3], beside[-2]),
            (sel.at[0], near_far.at[0], beside[1]),
            (sel.at[1], near_far.at[1], beside[-1]),
            (sel.at[1], other.at[0], beside[1]),
            (sel.at[0], other.at[1], beside[-1]),
        ]
        return [
            remote(src, dst, kv_send.at[j, i], kv_recv.at[j, i], to)
            for i, (src, dst, to) in enumerate(pieces_of)
        ]

    k_copies = spread_window(0, k_sel, k_in, k_other)
    v_copies = spread_window(1, v_sel, v_in, v_other)
    started += k_copies + v_copies
    tell(0)

    loads[5].wait()
    spread = jnp.broadcast_to(owners_ref[...], (n_blocks, n_blocks)).T
    slot_of = lax.broadcasted_iota(jnp.int32, (n_blocks, n_blocks), 1)
    block_of = lax.broadcasted_iota(jnp.int32, (n_blocks, n_blocks), 0)
    inv_v[...] = jnp.max(jnp.where(spread == slot_of, block_of, 0), 0, keepdims=True)
    inv_copy = pltpu.make_async_copy(inv_v, inv_s, load_sem.at[9])
    inv_copy.start()

    for load in loads[6:]:
        load.wait()
    xt_v[...] = x_v[...].T
    inv_copy.wait()

    key_row = lax.broadcasted_iota(jnp.int32, (half, half), 0)
    query_col = lax.broadcasted_iota(jnp.int32, (half, half), 1)
    queries = [q_ref[slot * half : (slot + 1) * half, :] for slot in range(2)]
    grads = [g_ref[slot * half : (slot + 1) * half, :] for slot in range(2)]
    by_row = ((1,), (1,))
    scores_own = [contract(k_own[slot], queries[slot], by_row) for slot in range(2)]
    dprob_own = [contract(v_own[slot], grads[slot], by_row) for slot in range(2)]

    def before(slot, own, near_far, other):
        if slot == 0:
            blocks = [near_far[jnp.where(up, 0, 1)], near_far[jnp.where(up, 2, 3)]]
        else:
            blocks = [
                jnp.where(last, own[0], near_far[jnp.where(up, 1, 0)]),
                jnp.where(
                    second_last,
                    other[jnp.where(up, 1, 0)],
                    near_far[jnp.where(last, jnp.where(up, 0, 1), jnp.where(up, 3, 2))],
                ),
            ]
        return jnp.concatenate(blocks, 0)

    def send_terms(j, these, terms, terms_in):
        copies = [
            remote(
                terms.at[these, pl.ds(pl.multiple_of(lax.rem(mate(0, b), n_x) * cut, cut), cut), :],
                terms_in.at[i, these],
                rs_send.at[j, i],
                rs_recv.at[j, i],
                (s, mate(0, b)),
            )
            for i, b in enumerate(along_x)
        ]
        started.extend(copies)
        return copies

    heard(0)
    for i in range(1, min(2, len(rounds))):
        tell(i)
    for copy in k_copies:
        copy.wait_recv()
    windows = [before(slot, k_own, k_in, k_other) for slot in range(2)]
    probs = []
    probs_b = []
    for slot in range(2):
        position = first if slot == 0 else 2 * n_seq - 1 - first
        visible = jnp.concatenate(
            [
                query_col >= key_row,
                jnp.broadcast_to(position >= 1, (half, half)),
                (query_col < key_row) & (position >= 2),
            ],
            0,
        )
        scores = jnp.concatenate(
            [scores_own[slot], contract(windows[slot], queries[slot], by_row)], 0
        )
        scores = jnp.where(visible, scores * score_scale, MASKED)
        top = jnp.max(scores, 0, keepdims=True)
        raw = jnp.exp(scores - top)
        probs.append(raw * (1.0 / jnp.sum(raw, 0, keepdims=True)))
        probs_b.append(probs[slot].astype(BF16))
        value_grad = contract(probs_b[slot], grads[slot], ((1,), (0,))).astype(BF16)
        terms_v[3 * slot : 3 * slot + 3] = value_grad.reshape(3, half, hd)
    rs_v_copies = send_terms(0, pl.ds(0, 6), terms_v, terms_v_in)

    for copy in v_copies:
        copy.wait_recv()
    dscores = []
    rs_k_copies = []
    for slot in range(2):
        values = before(slot, v_own, v_in, v_other)
        dprob = jnp.concatenate([dprob_own[slot], contract(values, grads[slot], by_row)], 0)
        delta = jnp.sum(probs_b[slot].astype(F32) * dprob, 0, keepdims=True)
        dscores.append((probs[slot] * (dprob - delta)).astype(BF16))
        key_grad = contract(dscores[slot], queries[slot], ((1,), (0,))).astype(BF16)
        terms_k[3 * slot : 3 * slot + 3] = key_grad.reshape(3, half, hd)
        rs_k_copies.append(send_terms(1 + slot, pl.ds(3 * slot, 3), terms_k, terms_k_in))

    for i in range(1, min(2, len(rounds))):
        heard(i)
    for i in range(2, len(rounds)):
        tell(i)
    for slot in range(2):
        query_grad = contract(dscores[slot][:half], k_own[slot], ((0,), (0,)))
        query_grad += contract(dscores[slot][half:], windows[slot], ((0,), (0,)))
        qg_ref[slot * half : (slot + 1) * half, :] = (query_grad * score_scale).astype(BF16)
    qg_copy = pltpu.make_async_copy(qg_ref, qg_hbm, load_sem.at[10])
    qg_copy.start()

    my_rows = pl.ds(pl.multiple_of(lax.rem(m, n_x) * cut, cut), cut)

    def head_sum(copies, terms, terms_in):
        total = terms[:, my_rows, :].astype(F32)
        for i in reversed(range(n_x - 1)):
            for part in copies:
                part[i].wait_recv()
            total = total + terms_in[i].astype(F32)
        return total

    def give_back(j, total):
        own0, down1, down2, own1, up1, up2 = [total[i] for i in range(6)]
        own0 = own0 + jnp.where(last, up1, 0.0)
        down1 = down1 + jnp.where(last, up2, 0.0)
        up1 = jnp.where(last, 0.0, up1)
        across = jnp.where(second_last, up2, 0.0)
        up2 = jnp.where(last | second_last, 0.0, up2)
        nothing = jnp.zeros_like(own0)
        pass_near[j, 0, 0] = jnp.where(up, across, down1).astype(BF16)
        pass_near[j, 0, 1] = jnp.where(up, up1, nothing).astype(BF16)
        pass_near[j, 1, 0] = jnp.where(up, down1, across).astype(BF16)
        pass_near[j, 1, 1] = jnp.where(up, nothing, up1).astype(BF16)
        pass_far[j, 0] = jnp.where(up, up2, down2).astype(BF16)
        pass_far[j, 1] = jnp.where(up, down2, up2).astype(BF16)
        kept[j, 0] = own0
        kept[j, 1] = own1
        own_out[j] = kept[j].astype(BF16)
        returns = [
            (pass_far.at[j, 0], pass_far_in.at[j, 0], place(2), 0),
            (pass_far.at[j, 1], pass_far_in.at[j, 1], place(-2), 1),
            (pass_near.at[j, 0], pass_near_in.at[j, 0], place(1), 2),
            (pass_near.at[j, 1], pass_near_in.at[j, 1], place(-1), 3),
            (own_out.at[j], own_in.at[j], s, 4),
        ]
        copies = [
            remote(src, dst.at[a], pass_send.at[j, i, a], pass_recv.at[j, i, a], (to, mate(a, 0)))
            for a in reversed(range(n_y))
            for src, dst, to, i in returns
            if a > 0 or i < 4
        ]
        started.extend(copies)
        return copies

    def gather(j, copies):
        for copy in copies:
            copy.wait_recv()
        total = kept[j]
        far_before = far_after = 0.0
        for a in range(n_y):
            total = total + pass_near_in[j, 0, a].astype(F32) + pass_near_in[j, 1, a].astype(F32)
            far_before = far_before + pass_far_in[j, 0, a].astype(F32)
            far_after = far_after + pass_far_in[j, 1, a].astype(F32)
            if a > 0:
                total = total + own_in[j, a].astype(F32)
        fin[j, 0] = (total[0] + jnp.where(up, far_after, far_before)).astype(BF16)
        fin[j, 1] = (total[1] + jnp.where(up, far_before, far_after)).astype(BF16)
        kvg[j, :, my_rows, :] = fin[j]
        copies = [
            remote(
                fin.at[j],
                kvg.at[j, :, my_rows, :],
                ag_send.at[j, i],
                ag_recv.at[j, i],
                (s, mate(0, b)),
            )
            for i, b in enumerate(along_x)
        ]
        started.extend(copies)
        return copies

    total_v = head_sum([rs_v_copies], terms_v, terms_v_in)
    pass_v_copies = give_back(1, total_v)
    total_k = head_sum(rs_k_copies, terms_k, terms_k_in) * score_scale
    pass_k_copies = give_back(0, total_k)
    ag_v_copies = gather(1, pass_v_copies)
    ag_k_copies = gather(0, pass_k_copies)

    lane = lax.broadcasted_iota(jnp.int32, (BLK // 2, 2 * BLK), 1)
    step = min(STEP, n_blocks // 4)
    for j, copies in ((1, ag_v_copies), (0, ag_k_copies)):
        for copy in copies:
            copy.wait_recv()
        kv_grad = kvg[j].reshape(rows, hd)
        for i in range(n_blocks // (4 * step)):
            part = contract(xt_v[i * step * BLK : (i + 1) * step * BLK, :], kv_grad, ((1,), (0,)))
            for r in range(step):
                tile = part[r * BLK : (r + 1) * BLK]
                upper, lower = tile[: BLK // 2], tile[BLK // 2 :]
                block = (i * step + r) * 4 + 2 * j
                pieces[block] = jnp.where(lane < BLK, upper, pltpu.roll(lower, BLK, 1))
                pieces[block + 1] = jnp.where(lane < BLK, pltpu.roll(upper, BLK, 1), lower)

    def owner_piece(p, whose_y, whose_core):
        t = n_z // 2 + (p + 1) // 2 * (1 - 2 * (p % 2))
        slot = 2 * (2 * lax.rem(z + t, n_z) + whose_y) + whose_core
        return pieces[inv_s[0, slot] & (n_blocks - 1)]

    n_parts = min(PARTS, n_z // 2)
    part = n_z // n_parts
    far_copies = []
    for g, (dy, dc) in enumerate([(1, 1), (1, 0), (0, 1)]):
        to_y, to_core = lax.rem(y + dy, 2), lax.rem(core + dc, 2)
        for p in range(part):
            far_out[g, p] = owner_piece(p, to_y, to_core).astype(BF16)
        far_copies.append(
            remote(
                far_out.at[g],
                far_in.at[g],
                far_send.at[g],
                far_recv.at[g],
                (4 * z + 2 * to_y + to_core, m),
            )
        )
    core_copies = {}
    for k, whose_y in enumerate((1 - y, y)):
        for c in range(1, n_parts):
            for p in range(c * part, (c + 1) * part):
                core_out[k, p] = owner_piece(p, whose_y, 1 - core).astype(BF16)
            here = pl.ds(c * part, part)
            core_copies[k, c] = remote(
                core_out.at[k, here],
                core_in.at[k, here],
                core_send.at[k, c],
                core_recv.at[k, c],
                (s + 1 - 2 * core, m),
            )
    for p in range(part, n_z):
        keep[0, p] = owner_piece(p, 1 - y, core)
    for p in range(n_z):
        keep[1, p] = owner_piece(p, y, core)

    y_copies = {}
    for c in range(1, n_parts):
        here = pl.ds(c * part, part)
        core_copies[0, c].wait_recv()
        y_out[here] = (keep[0, here] + core_in[0, here].astype(F32)).astype(BF16)
        y_copies[c] = remote(
            y_out.at[here], y_in.at[here], y_send.at[c], y_recv.at[c], (s + 2 - 4 * y, m)
        )
    for i in range(2, len(rounds)):
        heard(i)
    z_copies = []
    for c in range(n_parts):
        here = pl.ds(c * part, part)
        ours = keep[1, here]
        if c == 0:
            for g in (2, 1, 0):
                far_copies[g].wait_recv()
                ours = ours + far_in[g].astype(F32)
        else:
            core_copies[1, c].wait_recv()
            ours = ours + core_in[1, here].astype(F32)
            y_copies[c].wait_recv()
            ours = ours + y_in[here].astype(F32)
        z_out[here] = ours.astype(BF16)
        for p in range(c * part, min((c + 1) * part, n_z - 1)):
            t = n_z // 2 + (p + 1) // 2 * (1 - 2 * (p % 2))
            z_copies.append(
                remote(z_out.at[p], z_in.at[p], z_send.at[p], z_recv.at[p], (place(4 * t), m))
            )
    for copy in [*started, *far_copies, *core_copies.values(), *y_copies.values()]:
        copy.wait_send()
    qg_copy.wait()
    owned = ours[part - 1]
    for p in reversed(range(n_z - 1)):
        z_copies[p].wait_recv()
        owned = owned + z_in[p].astype(F32)
    sum_ref[...] = owned
    for copy in z_copies:
        copy.wait_send()


def finish(weight_scale, qg_ref, sum_ref, qg_out, block_out, left_out, right_out):
    qg_out[...] = qg_ref[...]
    owned = sum_ref[...] * weight_scale
    block = jnp.concatenate([owned[:, :BLK], owned[:, BLK:]], 0)
    block_out[0, 0] = block

    def exact(dims):
        return (
            lax.dot_general(
                block,
                block,
                (dims, ((), ())),
                precision=lax.Precision.HIGHEST,
                preferred_element_type=F32,
            )
            / BLK
        )

    left_out[0, 0] = exact(((1,), (1,)))
    right_out[0, 0] = exact(((0,), (0,)))


def shards(n_seq, n_mp, layer_input, query_heads, key_head, value_head, attn_grad, block_order, owners):
    rows, columns = layer_input.shape
    half = rows // 2
    hd = key_head.shape[1]
    n_x = min(4, n_mp)
    n_y = n_mp // n_x
    cut = half // n_x
    n_z = n_seq // 4
    n_blocks = owners.shape[1]
    shape = (BLK // 2, 2 * BLK)
    vmem = pl.BlockSpec(memory_space=pltpu.VMEM)
    stat = jax.ShapeDtypeStruct((1, 1, BLK, BLK), F32)
    dma = pltpu.SemaphoreType.DMA
    query_part = jax.ShapeDtypeStruct((rows, hd), BF16)
    query_grad, owned = pl.pallas_call(
        functools.partial(kernel, n_seq, n_mp),
        out_shape=(query_part, jax.ShapeDtypeStruct(shape, F32)),
        in_specs=[pl.BlockSpec(memory_space=pl.ANY)] * 7,
        out_specs=(pl.BlockSpec(memory_space=pl.ANY), vmem),
        scratch_shapes=[
            pltpu.VMEM((rows, hd), BF16),
            pltpu.SMEM((2 * n_seq,), jnp.int32),
            pltpu.VMEM((1, n_blocks), jnp.int32),
            pltpu.VMEM((rows, hd), BF16),
            pltpu.VMEM((rows, hd), BF16),
            pltpu.VMEM((rows, columns), BF16),
            pltpu.VMEM((columns, rows), BF16),
            pltpu.VMEM((1, n_blocks), jnp.int32),
            pltpu.SMEM((1, n_blocks), jnp.int32),
            pltpu.VMEM((2, half, hd), BF16),
            pltpu.VMEM((2, half, hd), BF16),
            pltpu.VMEM((4, half, hd), BF16),
            pltpu.VMEM((2, half, hd), BF16),
            pltpu.VMEM((2, half, hd), BF16),
            pltpu.VMEM((2, half, hd), BF16),
            pltpu.VMEM((4, half, hd), BF16),
            pltpu.VMEM((2, half, hd), BF16),
            pltpu.VMEM((6, half, hd), BF16),
            pltpu.VMEM((6, half, hd), BF16),
            pltpu.VMEM((n_x - 1, 6, cut, hd), BF16),
            pltpu.VMEM((n_x - 1, 6, cut, hd), BF16),
            pltpu.VMEM((2, 2, 2, cut, hd), BF16),
            pltpu.VMEM((2, 2, cut, hd), BF16),
            pltpu.VMEM((2, 2, n_y, 2, cut, hd), BF16),
            pltpu.VMEM((2, 2, n_y, cut, hd), BF16),
            pltpu.VMEM((2, 2, cut, hd), BF16),
            pltpu.VMEM((2, n_y, 2, cut, hd), BF16),
            pltpu.VMEM((2, 2, cut, hd), F32),
            pltpu.VMEM((2, 2, cut, hd), BF16),
            pltpu.VMEM((2, 2, half, hd), BF16),
            pltpu.VMEM((n_blocks, *shape), F32),
            pltpu.VMEM((2, n_z, *shape), F32),
            pltpu.VMEM((3, n_z // min(PARTS, n_z // 2), *shape), BF16),
            pltpu.VMEM((3, n_z // min(PARTS, n_z // 2), *shape), BF16),
            pltpu.VMEM((2, n_z, *shape), BF16),
            pltpu.VMEM((2, n_z, *shape), BF16),
            pltpu.VMEM((n_z, *shape), BF16),
            pltpu.VMEM((n_z, *shape), BF16),
            pltpu.VMEM((n_z, *shape), BF16),
            pltpu.VMEM((n_z - 1, *shape), BF16),
            dma((11,)),
            pltpu.SemaphoreType.REGULAR((4,)),
            dma((2, 6)),
            dma((2, 6)),
            dma((3, n_x - 1)),
            dma((3, n_x - 1)),
            dma((2, 5, n_y)),
            dma((2, 5, n_y)),
            dma((2, n_x - 1)),
            dma((2, n_x - 1)),
            dma((3,)),
            dma((3,)),
            dma((2, PARTS)),
            dma((2, PARTS)),
            dma((PARTS,)),
            dma((PARTS,)),
            dma((n_z - 1,)),
            dma((n_z - 1,)),
        ],
        compiler_params=pltpu.CompilerParams(
            collective_id=0, has_side_effects=True, vmem_limit_bytes=60 * 1024 * 1024
        ),
    )(block_order, owners, layer_input, query_heads, key_head, value_head, attn_grad)
    return pl.pallas_call(
        functools.partial(finish, 1.0 / math.sqrt(rows * n_seq)),
        out_shape=(query_part, stat, stat, stat),
        in_specs=[vmem, vmem],
        out_specs=(vmem, vmem, vmem, vmem),
        compiler_params=pltpu.CompilerParams(vmem_limit_bytes=60 * 1024 * 1024),
    )(query_grad, owned)


def solution(mesh):
    return jax.shard_map(
        functools.partial(shards, mesh.shape["seq"], mesh.shape["mp"]),
        mesh=mesh,
        in_specs=(
            P("seq", "mp"),
            P("seq", "mp"),
            P("seq", None),
            P("seq", None),
            P("seq", "mp"),
            P(),
            P("mp", None),
        ),
        out_specs=(
            P("seq", "mp"),
            P("mp", "seq", None, None),
            P("mp", "seq", None, None),
            P("mp", "seq", None, None),
        ),
        check_vma=False,
    )
```

```python
import functools
import math

import jax
import jax.numpy as jnp
from jax import lax
from jax.experimental import pallas as pl
from jax.experimental.pallas import tpu as pltpu
from jax.sharding import PartitionSpec as P

BLK = 64
STEP = 4
PARTS = 4
MASKED = -1e30
MESH = pl.DeviceIdType.MESH
F32 = jnp.float32
BF16 = jnp.bfloat16


def contract(a, b, dims):
    return lax.dot_general(a, b, (dims, ((), ())), preferred_element_type=F32)


def kernel(
    n_seq,
    n_mp,
    order_hbm,
    owners_hbm,
    x_hbm,
    q_hbm,
    k_hbm,
    v_hbm,
    g_hbm,
    qg_hbm,
    sum_ref,
    qg_ref,
    order_ref,
    owners_ref,
    q_ref,
    g_ref,
    x_v,
    xt_v,
    inv_v,
    inv_s,
    k_own,
    k_sel,
    k_in,
    k_other,
    v_own,
    v_sel,
    v_in,
    v_other,
    terms_k,
    terms_v,
    terms_k_in,
    terms_v_in,
    pass_near,
    pass_far,
    pass_near_in,
    pass_far_in,
    own_out,
    own_in,
    kept,
    fin,
    kvg,
    pieces,
    keep,
    far_out,
    far_in,
    core_out,
    core_in,
    y_out,
    y_in,
    z_out,
    z_in,
    load_sem,
    word_sem,
    kv_send,
    kv_recv,
    rs_send,
    rs_recv,
    pass_send,
    pass_recv,
    ag_send,
    ag_recv,
    far_send,
    far_recv,
    core_send,
    core_recv,
    y_send,
    y_recv,
    z_send,
    z_recv,
):
    n_z = n_seq // 4
    rows = q_ref.shape[0]
    half = rows // 2
    hd = q_ref.shape[1]
    n_x = min(4, n_mp)
    n_y = n_mp // n_x
    cut = half // n_x
    n_blocks = pieces.shape[0]
    score_scale = 1.0 / math.sqrt(hd)

    s = lax.axis_index("seq")
    m = lax.axis_index("mp")
    core = lax.rem(s, 2)
    y = lax.rem(s // 2, 2)
    z = s // 4

    def place(distance):
        return lax.rem(s + distance + n_seq, n_seq)

    def mate(a, b):
        return lax.rem(m // n_x + a, n_y) * n_x + lax.rem(lax.rem(m, n_x) + b, n_x)

    along_x = sorted(range(1, n_x), key=lambda b: -min(b, n_x - b))

    barrier = pltpu.get_barrier_semaphore()
    next_z = [(place(4 * t), m) for t in sorted({1, n_z - 1})]
    crossing = {2: y, -2: 1 - y, 1: core * y, -1: (1 - core) * (1 - y)}
    beside = {d: (place(d), lax.rem(m + cross * n_x, n_mp)) for d, cross in crossing.items()}
    partners = list(beside.values()) + next_z
    partners += [(s, mate(0, b)) for b in along_x] + [(s, mate(a, 0)) for a in range(1, n_y)]
    reaches = [1 << i for i in range((n_z // 2).bit_length() - 1)]
    along_z = [[(place(4 * t), m) for t in (r, n_z - r)] for r in reaches[1:]]
    rounds = [partners, *along_z]

    def tell(i):
        for partner in rounds[i]:
            pl.semaphore_signal(
                word_sem.at[i], inc=1, device_id=partner, device_id_type=MESH
            )

    def heard(i):
        pl.semaphore_wait(word_sem.at[i], len(rounds[i]))

    for partner in partners:
        pl.semaphore_signal(barrier, inc=1, device_id=partner, device_id_type=MESH)

    loads = [
        pltpu.make_async_copy(src, dst, load_sem.at[i])
        for i, (src, dst) in enumerate(
            [
                (order_hbm, order_ref),
                (k_hbm.at[0:half], k_own.at[0]),
                (v_hbm.at[0:half], v_own.at[0]),
                (k_hbm.at[half:rows], k_own.at[1]),
                (v_hbm.at[half:rows], v_own.at[1]),
                (owners_hbm, owners_ref),
                (q_hbm, q_ref),
                (g_hbm, g_ref),
                (x_hbm, x_v),
            ]
        )
    ]
    for load in loads:
        load.start()

    for load in loads[:5]:
        load.wait()

    first = order_ref[2 * s]
    following = order_ref[2 * place(1)]
    up = ((following - first + n_seq) & (n_seq - 1)) == 1
    last = first == n_seq - 1
    second_last = first == n_seq - 2

    for own, sel in ((k_own, k_sel), (v_own, v_sel)):
        sel[0] = own[jnp.where(up, 0, 1)]
        sel[1] = own[jnp.where(up, 1, 0)]

    pl.semaphore_wait(barrier, len(partners))

    def remote(src, dst, send_sem, recv_sem, to):
        copy = pltpu.make_async_remote_copy(
            src_ref=src,
            dst_ref=dst,
            send_sem=send_sem,
            recv_sem=recv_sem,
            device_id=to,
            device_id_type=MESH,
        )
        copy.start()
        return copy

    started = []
    def spread_window(j, sel, near_far, other):
        pieces_of = [
            (sel.at[0], near_far.at[2], beside[2]),
            (sel.at[1], near_far.at[3], beside[-2]),
            (sel.at[0], near_far.at[0], beside[1]),
            (sel.at[1], near_far.at[1], beside[-1]),
            (sel.at[1], other.at[0], beside[1]),
            (sel.at[0], other.at[1], beside[-1]),
        ]
        return [
            remote(src, dst, kv_send.at[j, i], kv_recv.at[j, i], to)
            for i, (src, dst, to) in enumerate(pieces_of)
        ]

    k_copies = spread_window(0, k_sel, k_in, k_other)
    v_copies = spread_window(1, v_sel, v_in, v_other)
    started += k_copies + v_copies
    tell(0)

    loads[5].wait()
    spread = jnp.broadcast_to(owners_ref[...], (n_blocks, n_blocks)).T
    slot_of = lax.broadcasted_iota(jnp.int32, (n_blocks, n_blocks), 1)
    block_of = lax.broadcasted_iota(jnp.int32, (n_blocks, n_blocks), 0)
    inv_v[...] = jnp.max(jnp.where(spread == slot_of, block_of, 0), 0, keepdims=True)
    inv_copy = pltpu.make_async_copy(inv_v, inv_s, load_sem.at[9])
    inv_copy.start()

    for load in loads[6:]:
        load.wait()
    xt_v[...] = x_v[...].T
    inv_copy.wait()

    key_row = lax.broadcasted_iota(jnp.int32, (half, half), 0)
    query_col = lax.broadcasted_iota(jnp.int32, (half, half), 1)
    queries = [q_ref[slot * half : (slot + 1) * half, :] for slot in range(2)]
    grads = [g_ref[slot * half : (slot + 1) * half, :] for slot in range(2)]
    by_row = ((1,), (1,))
    scores_own = [contract(k_own[slot], queries[slot], by_row) for slot in range(2)]
    dprob_own = [contract(v_own[slot], grads[slot], by_row) for slot in range(2)]

    def before(slot, own, near_far, other):
        if slot == 0:
            blocks = [near_far[jnp.where(up, 0, 1)], near_far[jnp.where(up, 2, 3)]]
        else:
            blocks = [
                jnp.where(last, own[0], near_far[jnp.where(up, 1, 0)]),
                jnp.where(
                    second_last,
                    other[jnp.where(up, 1, 0)],
                    near_far[jnp.where(last, jnp.where(up, 0, 1), jnp.where(up, 3, 2))],
                ),
            ]
        return jnp.concatenate(blocks, 0)

    def send_terms(j, these, terms, terms_in):
        copies = [
            remote(
                terms.at[these, pl.ds(pl.multiple_of(lax.rem(mate(0, b), n_x) * cut, cut), cut), :],
                terms_in.at[i, these],
                rs_send.at[j, i],
                rs_recv.at[j, i],
                (s, mate(0, b)),
            )
            for i, b in enumerate(along_x)
        ]
        started.extend(copies)
        return copies

    heard(0)
    for i in range(1, min(2, len(rounds))):
        tell(i)
    for copy in k_copies:
        copy.wait_recv()
    windows = [before(slot, k_own, k_in, k_other) for slot in range(2)]
    probs = []
    probs_b = []
    for slot in range(2):
        position = first if slot == 0 else 2 * n_seq - 1 - first
        visible = jnp.concatenate(
            [
                query_col >= key_row,
                jnp.broadcast_to(position >= 1, (half, half)),
                (query_col < key_row) & (position >= 2),
            ],
            0,
        )
        scores = jnp.concatenate(
            [scores_own[slot], contract(windows[slot], queries[slot], by_row)], 0
        )
        scores = jnp.where(visible, scores * score_scale, MASKED)
        top = jnp.max(scores, 0, keepdims=True)
        raw = jnp.exp(scores - top)
        probs.append(raw * (1.0 / jnp.sum(raw, 0, keepdims=True)))
        probs_b.append(probs[slot].astype(BF16))
        value_grad = contract(probs_b[slot], grads[slot], ((1,), (0,))).astype(BF16)
        terms_v[3 * slot : 3 * slot + 3] = value_grad.reshape(3, half, hd)
    rs_v_copies = send_terms(0, pl.ds(0, 6), terms_v, terms_v_in)

    for copy in v_copies:
        copy.wait_recv()
    dscores = []
    rs_k_copies = []
    for slot in range(2):
        values = before(slot, v_own, v_in, v_other)
        dprob = jnp.concatenate([dprob_own[slot], contract(values, grads[slot], by_row)], 0)
        delta = jnp.sum(probs_b[slot].astype(F32) * dprob, 0, keepdims=True)
        dscores.append((probs[slot] * (dprob - delta)).astype(BF16))
        key_grad = contract(dscores[slot], queries[slot], ((1,), (0,))).astype(BF16)
        terms_k[3 * slot : 3 * slot + 3] = key_grad.reshape(3, half, hd)
        rs_k_copies.append(send_terms(1 + slot, pl.ds(3 * slot, 3), terms_k, terms_k_in))

    for i in range(1, min(2, len(rounds))):
        heard(i)
    for i in range(2, len(rounds)):
        tell(i)
    for slot in range(2):
        query_grad = contract(dscores[slot][:half], k_own[slot], ((0,), (0,)))
        query_grad += contract(dscores[slot][half:], windows[slot], ((0,), (0,)))
        qg_ref[slot * half : (slot + 1) * half, :] = (query_grad * score_scale).astype(BF16)
    qg_copy = pltpu.make_async_copy(qg_ref, qg_hbm, load_sem.at[10])
    qg_copy.start()

    my_rows = pl.ds(pl.multiple_of(lax.rem(m, n_x) * cut, cut), cut)

    def head_sum(copies, terms, terms_in):
        total = terms[:, my_rows, :].astype(F32)
        for i in reversed(range(n_x - 1)):
            for part in copies:
                part[i].wait_recv()
            total = total + terms_in[i].astype(F32)
        return total

    def give_back(j, total):
        own0, down1, down2, own1, up1, up2 = [total[i] for i in range(6)]
        own0 = own0 + jnp.where(last, up1, 0.0)
        down1 = down1 + jnp.where(last, up2, 0.0)
        up1 = jnp.where(last, 0.0, up1)
        across = jnp.where(second_last, up2, 0.0)
        up2 = jnp.where(last | second_last, 0.0, up2)
        nothing = jnp.zeros_like(own0)
        pass_near[j, 0, 0] = jnp.where(up, across, down1).astype(BF16)
        pass_near[j, 0, 1] = jnp.where(up, up1, nothing).astype(BF16)
        pass_near[j, 1, 0] = jnp.where(up, down1, across).astype(BF16)
        pass_near[j, 1, 1] = jnp.where(up, nothing, up1).astype(BF16)
        pass_far[j, 0] = jnp.where(up, up2, down2).astype(BF16)
        pass_far[j, 1] = jnp.where(up, down2, up2).astype(BF16)
        kept[j, 0] = own0
        kept[j, 1] = own1
        own_out[j] = kept[j].astype(BF16)
        returns = [
            (pass_far.at[j, 0], pass_far_in.at[j, 0], place(2), 0),
            (pass_far.at[j, 1], pass_far_in.at[j, 1], place(-2), 1),
            (pass_near.at[j, 0], pass_near_in.at[j, 0], place(1), 2),
            (pass_near.at[j, 1], pass_near_in.at[j, 1], place(-1), 3),
            (own_out.at[j], own_in.at[j], s, 4),
        ]
        copies = [
            remote(src, dst.at[a], pass_send.at[j, i, a], pass_recv.at[j, i, a], (to, mate(a, 0)))
            for a in reversed(range(n_y))
            for src, dst, to, i in returns
            if a > 0 or i < 4
        ]
        started.extend(copies)
        return copies

    def gather(j, copies):
        for copy in copies:
            copy.wait_recv()
        total = kept[j]
        far_before = far_after = 0.0
        for a in range(n_y):
            total = total + pass_near_in[j, 0, a].astype(F32) + pass_near_in[j, 1, a].astype(F32)
            far_before = far_before + pass_far_in[j, 0, a].astype(F32)
            far_after = far_after + pass_far_in[j, 1, a].astype(F32)
            if a > 0:
                total = total + own_in[j, a].astype(F32)
        fin[j, 0] = (total[0] + jnp.where(up, far_after, far_before)).astype(BF16)
        fin[j, 1] = (total[1] + jnp.where(up, far_before, far_after)).astype(BF16)
        kvg[j, :, my_rows, :] = fin[j]
        copies = [
            remote(
                fin.at[j],
                kvg.at[j, :, my_rows, :],
                ag_send.at[j, i],
                ag_recv.at[j, i],
                (s, mate(0, b)),
            )
            for i, b in enumerate(along_x)
        ]
        started.extend(copies)
        return copies

    total_v = head_sum([rs_v_copies], terms_v, terms_v_in)
    pass_v_copies = give_back(1, total_v)
    total_k = head_sum(rs_k_copies, terms_k, terms_k_in) * score_scale
    pass_k_copies = give_back(0, total_k)
    ag_v_copies = gather(1, pass_v_copies)
    ag_k_copies = gather(0, pass_k_copies)

    lane = lax.broadcasted_iota(jnp.int32, (BLK // 2, 2 * BLK), 1)
    step = min(STEP, n_blocks // 4)
    for j, copies in ((1, ag_v_copies), (0, ag_k_copies)):
        for copy in copies:
            copy.wait_recv()
        kv_grad = kvg[j].reshape(rows, hd)
        for i in range(n_blocks // (4 * step)):
            part = contract(xt_v[i * step * BLK : (i + 1) * step * BLK, :], kv_grad, ((1,), (0,)))
            for r in range(step):
                tile = part[r * BLK : (r + 1) * BLK]
                upper, lower = tile[: BLK // 2], tile[BLK // 2 :]
                block = (i * step + r) * 4 + 2 * j
                pieces[block] = jnp.where(lane < BLK, upper, pltpu.roll(lower, BLK, 1))
                pieces[block + 1] = jnp.where(lane < BLK, pltpu.roll(upper, BLK, 1), lower)

    def owner_piece(p, whose_y, whose_core):
        t = n_z // 2 + (p + 1) // 2 * (1 - 2 * (p % 2))
        slot = 2 * (2 * lax.rem(z + t, n_z) + whose_y) + whose_core
        return pieces[inv_s[0, slot] & (n_blocks - 1)]

    n_parts = min(PARTS, n_z // 2)
    part = n_z // n_parts
    far_copies = []
    for g, (dy, dc) in enumerate([(1, 1), (1, 0), (0, 1)]):
        to_y, to_core = lax.rem(y + dy, 2), lax.rem(core + dc, 2)
        for p in range(part):
            far_out[g, p] = owner_piece(p, to_y, to_core).astype(BF16)
        far_copies.append(
            remote(
                far_out.at[g],
                far_in.at[g],
                far_send.at[g],
                far_recv.at[g],
                (4 * z + 2 * to_y + to_core, m),
            )
        )
    core_copies = {}
    for k, whose_y in enumerate((1 - y, y)):
        for c in range(1, n_parts):
            for p in range(c * part, (c + 1) * part):
                core_out[k, p] = owner_piece(p, whose_y, 1 - core).astype(BF16)
            here = pl.ds(c * part, part)
            core_copies[k, c] = remote(
                core_out.at[k, here],
                core_in.at[k, here],
                core_send.at[k, c],
                core_recv.at[k, c],
                (s + 1 - 2 * core, m),
            )
    for p in range(part, n_z):
        keep[0, p] = owner_piece(p, 1 - y, core)
    for p in range(n_z):
        keep[1, p] = owner_piece(p, y, core)

    y_copies = {}
    for c in range(1, n_parts):
        here = pl.ds(c * part, part)
        core_copies[0, c].wait_recv()
        y_out[here] = (keep[0, here] + core_in[0, here].astype(F32)).astype(BF16)
        y_copies[c] = remote(
            y_out.at[here], y_in.at[here], y_send.at[c], y_recv.at[c], (s + 2 - 4 * y, m)
        )
    for i in range(2, len(rounds)):
        heard(i)
    z_copies = []
    for c in range(n_parts):
        here = pl.ds(c * part, part)
        ours = keep[1, here]
        if c == 0:
            for g in (2, 1, 0):
                far_copies[g].wait_recv()
                ours = ours + far_in[g].astype(F32)
        else:
            core_copies[1, c].wait_recv()
            ours = ours + core_in[1, here].astype(F32)
            y_copies[c].wait_recv()
            ours = ours + y_in[here].astype(F32)
        z_out[here] = ours.astype(BF16)
        for p in range(c * part, min((c + 1) * part, n_z - 1)):
            t = n_z // 2 + (p + 1) // 2 * (1 - 2 * (p % 2))
            z_copies.append(
                remote(z_out.at[p], z_in.at[p], z_send.at[p], z_recv.at[p], (place(4 * t), m))
            )
    for copy in [*started, *far_copies, *core_copies.values(), *y_copies.values()]:
        copy.wait_send()
    qg_copy.wait()
    owned = ours[part - 1]
    for p in reversed(range(n_z - 1)):
        if p == 0:
            for copy in z_copies[1:]:
                copy.wait_send()
        z_copies[p].wait_recv()
        owned = owned + z_in[p].astype(F32)
    sum_ref[...] = owned
    z_copies[0].wait_send()


def finish(weight_scale, qg_ref, sum_ref, qg_out, block_out, left_out, right_out):
    qg_out[...] = qg_ref[...]
    owned = sum_ref[...] * weight_scale
    block = jnp.concatenate([owned[:, :BLK], owned[:, BLK:]], 0)
    block_out[0, 0] = block

    def exact(dims):
        return (
            lax.dot_general(
                block,
                block,
                (dims, ((), ())),
                precision=lax.Precision.HIGHEST,
                preferred_element_type=F32,
            )
            / BLK
        )

    left_out[0, 0] = exact(((1,), (1,)))
    right_out[0, 0] = exact(((0,), (0,)))


def shards(n_seq, n_mp, layer_input, query_heads, key_head, value_head, attn_grad, block_order, owners):
    rows, columns = layer_input.shape
    half = rows // 2
    hd = key_head.shape[1]
    n_x = min(4, n_mp)
    n_y = n_mp // n_x
    cut = half // n_x
    n_z = n_seq // 4
    n_blocks = owners.shape[1]
    shape = (BLK // 2, 2 * BLK)
    vmem = pl.BlockSpec(memory_space=pltpu.VMEM)
    stat = jax.ShapeDtypeStruct((1, 1, BLK, BLK), F32)
    dma = pltpu.SemaphoreType.DMA
    query_part = jax.ShapeDtypeStruct((rows, hd), BF16)
    query_grad, owned = pl.pallas_call(
        functools.partial(kernel, n_seq, n_mp),
        out_shape=(query_part, jax.ShapeDtypeStruct(shape, F32)),
        in_specs=[pl.BlockSpec(memory_space=pl.ANY)] * 7,
        out_specs=(pl.BlockSpec(memory_space=pl.ANY), vmem),
        scratch_shapes=[
            pltpu.VMEM((rows, hd), BF16),
            pltpu.SMEM((2 * n_seq,), jnp.int32),
            pltpu.VMEM((1, n_blocks), jnp.int32),
            pltpu.VMEM((rows, hd), BF16),
            pltpu.VMEM((rows, hd), BF16),
            pltpu.VMEM((rows, columns), BF16),
            pltpu.VMEM((columns, rows), BF16),
            pltpu.VMEM((1, n_blocks), jnp.int32),
            pltpu.SMEM((1, n_blocks), jnp.int32),
            pltpu.VMEM((2, half, hd), BF16),
            pltpu.VMEM((2, half, hd), BF16),
            pltpu.VMEM((4, half, hd), BF16),
            pltpu.VMEM((2, half, hd), BF16),
            pltpu.VMEM((2, half, hd), BF16),
            pltpu.VMEM((2, half, hd), BF16),
            pltpu.VMEM((4, half, hd), BF16),
            pltpu.VMEM((2, half, hd), BF16),
            pltpu.VMEM((6, half, hd), BF16),
            pltpu.VMEM((6, half, hd), BF16),
            pltpu.VMEM((n_x - 1, 6, cut, hd), BF16),
            pltpu.VMEM((n_x - 1, 6, cut, hd), BF16),
            pltpu.VMEM((2, 2, 2, cut, hd), BF16),
            pltpu.VMEM((2, 2, cut, hd), BF16),
            pltpu.VMEM((2, 2, n_y, 2, cut, hd), BF16),
            pltpu.VMEM((2, 2, n_y, cut, hd), BF16),
            pltpu.VMEM((2, 2, cut, hd), BF16),
            pltpu.VMEM((2, n_y, 2, cut, hd), BF16),
            pltpu.VMEM((2, 2, cut, hd), F32),
            pltpu.VMEM((2, 2, cut, hd), BF16),
            pltpu.VMEM((2, 2, half, hd), BF16),
            pltpu.VMEM((n_blocks, *shape), F32),
            pltpu.VMEM((2, n_z, *shape), F32),
            pltpu.VMEM((3, n_z // min(PARTS, n_z // 2), *shape), BF16),
            pltpu.VMEM((3, n_z // min(PARTS, n_z // 2), *shape), BF16),
            pltpu.VMEM((2, n_z, *shape), BF16),
            pltpu.VMEM((2, n_z, *shape), BF16),
            pltpu.VMEM((n_z, *shape), BF16),
            pltpu.VMEM((n_z, *shape), BF16),
            pltpu.VMEM((n_z, *shape), BF16),
            pltpu.VMEM((n_z - 1, *shape), BF16),
            dma((11,)),
            pltpu.SemaphoreType.REGULAR((4,)),
            dma((2, 6)),
            dma((2, 6)),
            dma((3, n_x - 1)),
            dma((3, n_x - 1)),
            dma((2, 5, n_y)),
            dma((2, 5, n_y)),
            dma((2, n_x - 1)),
            dma((2, n_x - 1)),
            dma((3,)),
            dma((3,)),
            dma((2, PARTS)),
            dma((2, PARTS)),
            dma((PARTS,)),
            dma((PARTS,)),
            dma((n_z - 1,)),
            dma((n_z - 1,)),
        ],
        compiler_params=pltpu.CompilerParams(
            collective_id=0, has_side_effects=True, vmem_limit_bytes=60 * 1024 * 1024
        ),
    )(block_order, owners, layer_input, query_heads, key_head, value_head, attn_grad)
    return pl.pallas_call(
        functools.partial(finish, 1.0 / math.sqrt(rows * n_seq)),
        out_shape=(query_part, stat, stat, stat),
        in_specs=[vmem, vmem],
        out_specs=(vmem, vmem, vmem, vmem),
        compiler_params=pltpu.CompilerParams(vmem_limit_bytes=60 * 1024 * 1024),
    )(query_grad, owned)


def solution(mesh):
    return jax.shard_map(
        functools.partial(shards, mesh.shape["seq"], mesh.shape["mp"]),
        mesh=mesh,
        in_specs=(
            P("seq", "mp"),
            P("seq", "mp"),
            P("seq", None),
            P("seq", None),
            P("seq", "mp"),
            P(),
            P("mp", None),
        ),
        out_specs=(
            P("seq", "mp"),
            P("mp", "seq", None, None),
            P("mp", "seq", None, None),
            P("mp", "seq", None, None),
        ),
        check_vma=False,
    )
```
